256 devices in a mesh: samp: 8 (over z_hi, x), site: 32 (over z_lo, y, core).
Axes of the slice: x: 4, y: 4, z: 8 (z_hi: 2, z_lo: 4; z = z_hi * 4 + z_lo), core: 2. Of those that a mesh axis runs over, the one named last changes fastest.
Arguments:
- ensemble: bfloat16 [32768, 32768], P('site', 'samp'), may hold values from -1500 to 1500
- probes: bfloat16 [32768, 512], P('samp'), may hold values from -0.03125 to 0.03125
- site_bus: int32 [1024], replicated, may hold values from 0 to 1023, as said below
- incidence: int32 [2048, 8], P(('samp', 'site')), may hold values from 0 to 1023, as said below
- shift_factors: bfloat16 [32768, 256], P(('samp', 'site')), may hold values from -0.375 to 0.375
Outputs:
- line_basis: float32 [32768, 512], P(('samp', 'site'))
The draws below stay inside these ranges and needn't reach their ends.
Inputs may be any that keep to these rules, and one draw needn't show every extreme that they name: `site_bus`: A permutation of the 1024 blocks; the 32 site blocks b * 32 to (b + 1) * 32 - 1 go to bus blocks of 32 different owners e (bus blocks e * 32 to (e + 1) * 32 - 1), one each. `incidence`: line l belongs to index i = (l // 128) % 32 of site; every entry of its group's list is a bus block of owner i - 1, i or i + 1 (modulo 32).
All inputs are finite; a program needn't handle non-finite values.
Results may differ from the reference program's by a relative error of at most 0.013.
Values sent between devices are 32-bit elements; how exact they have to be, the bound alone decides.
No kernel may reach another device: no remote copies, remote signals or barrier semaphores. Data moves between devices by JAX's collectives and lax.ppermute only.
A program may use at most 128 MiB of HBM per device.

```python
import math
import jax
import jax.numpy as jnp
from jax import lax

K = 512
SITE_DEV = 1024
LINE_DEV = 128
LBLK = 16
INC = 8
BPD = 32
BLOCK = 32
NBLK = 1024
SITES = 32768
SAMPLES = 32768
LINES = 32768
NLB = 2048


def draw_ensemble(key, part):
    key = jax.random.fold_in(key, 11)
    subkeys = jax.random.split(key, 6)
    noise_field = jnp.clip(jax.random.normal(subkeys[0], (SITES, SAMPLES), jnp.float32), -5.0, 5.0)
    row_scale = jnp.exp(jax.random.uniform(subkeys[1], (SITES, 1), jnp.float32) * math.log(2.0))
    shard_scale = jnp.exp(jax.random.uniform(subkeys[5], (SITES // SITE_DEV, 1, 1), jnp.float32) * math.log(5.0))
    shard_rows = jnp.broadcast_to(shard_scale, (SITES // SITE_DEV, SITE_DEV, 1)).reshape(SITES, 1)
    col_scale = jnp.exp(jax.random.uniform(subkeys[2], (1, SAMPLES), jnp.float32) * math.log(10.0))
    site_ramp = jnp.exp(math.log(3.0) * jnp.arange(SITES, dtype=jnp.float32)[:, None] / max(SITES - 1, 1))
    return (noise_field * row_scale * shard_rows * col_scale * site_ramp).astype(jnp.bfloat16)


def permute_one(sub_key):
    return jax.random.permutation(sub_key, BPD)


def draw_site_bus(key, part):
    key = jax.random.fold_in(key, 5)
    dest_key, slot_key = jax.random.split(key)
    targets = jax.vmap(permute_one)(jax.random.split(dest_key, BPD)).astype(jnp.int32)
    slots = jax.vmap(permute_one)(jax.random.split(slot_key, BPD)).astype(jnp.int32)
    sources = jnp.broadcast_to(jnp.arange(BPD, dtype=jnp.int32)[:, None], (BPD, BPD))
    slot_taken = slots[targets, sources]
    return (targets * BPD + slot_taken).reshape(NBLK).astype(jnp.int32)


def draw_incidence(key, part):
    key = jax.random.fold_in(key, 7)
    shift_key, block_key = jax.random.split(key)
    groups = jnp.arange(NLB, dtype=jnp.int32)
    owner_site = groups // (LINE_DEV // LBLK) % BPD
    offsets = jax.random.randint(shift_key, (NLB, INC), -1, 2, dtype=jnp.int32)
    picks = jax.random.randint(block_key, (NLB, INC), 0, BPD, dtype=jnp.int32)
    return ((owner_site[:, None] + offsets) % BPD * BPD + picks).astype(jnp.int32)


def level_of(own_key, extent, pieces, least, top_value):
    def one(dim, shards_of):
        heights = jax.random.uniform(jax.random.fold_in(jax.random.fold_in(own_key, 6), dim), (shards_of,), jnp.float32, least / len(pieces), top_value / len(pieces))
        return jnp.repeat(jnp.exp(heights), extent[dim] // shards_of).reshape((-1,) + (1,) * (len(extent) - dim - 1))

    gain = one(*pieces[0])
    for cut in pieces[1:]:
        gain = gain * one(*cut)
    return gain


def normal_values(key, extent, scale, limit, shards=(), held_as=jnp.bfloat16):
    values = scale * jax.random.normal(key, extent, jnp.float32)
    if shards:
        values = values * level_of(key, extent, shards, -0.22, 0.18)
    return jnp.clip(values, -limit, limit).astype(held_as)


def setup_inputs(seed: int = 0) -> dict:
    arg_keys = jax.random.split(jax.random.key(seed), 6)
    return {
        "ensemble": draw_ensemble(jax.random.fold_in(arg_keys[5], 71), 0),
        "probes": normal_values(arg_keys[1], (SAMPLES, K), SAMPLES ** -0.5, 0.03125, ((0, 8),)),
        "site_bus": draw_site_bus(jax.random.fold_in(arg_keys[5], 71), 0),
        "incidence": draw_incidence(jax.random.fold_in(arg_keys[5], 71), 0),
        "shift_factors": normal_values(arg_keys[4], (LINES, INC * BLOCK), (INC * BLOCK) ** -0.5, 0.375, ((0, 256),)),
    }


def reference(ensemble, probes, site_bus, incidence, shift_factors):
    sketch = jnp.dot(ensemble.astype(jnp.float32), probes.astype(jnp.float32), preferred_element_type=jnp.float32)
    gram = jnp.dot(sketch.T, sketch, precision=lax.Precision.HIGHEST)
    factor = jnp.linalg.cholesky(gram)
    solved = jax.scipy.linalg.solve_triangular(factor, sketch.T, lower=True).T
    basis = solved * math.sqrt(SITES)
    blocks = basis.reshape(NBLK, BLOCK, K)
    bus_blocks = jnp.zeros_like(blocks).at[site_bus].set(blocks)

    def one_group(group_pair):
        factors_group, links_group = group_pair
        chosen = bus_blocks[links_group].reshape(INC * BLOCK, K)
        return jnp.dot(factors_group.astype(jnp.float32), chosen, precision=lax.Precision.HIGHEST)
    grouped = lax.map(one_group, (shift_factors.reshape(NLB, LBLK, INC * BLOCK), incidence))
    return grouped.reshape(LINES, K)
```

```python
import functools
import math

import jax
import jax.numpy as jnp
from jax import lax
from jax.experimental import pallas as pl
from jax.experimental.pallas import tpu as pltpu
from jax.sharding import PartitionSpec as P

FULL = lax.Precision.HIGHEST
F32 = jnp.float32
NX = 4
NZL = 4
NY = 4
NC = 2
UPPER = ((0, 0), (0, 1), (0, 2), (0, 3), (3, 3), (1, 1), (1, 2), (1, 3), (2, 2), (2, 3))
VMEM = pl.BlockSpec(memory_space=pltpu.VMEM)
SMEM = pl.BlockSpec(memory_space=pltpu.SMEM)


def params(mib=48):
    return pltpu.CompilerParams(vmem_limit_bytes=mib * 1024 * 1024)


def cost(flops, moved):
    return pl.CostEstimate(flops=flops, bytes_accessed=moved, transcendentals=0)


def shift_x(value, step):
    pairs = [(h * NX + x, h * NX + (x + step) % NX) for h in range(2) for x in range(NX)]
    return lax.ppermute(value, "samp", pairs)


def swap_half(value):
    return lax.ppermute(value, "samp", [(s, (s + NX) % (2 * NX)) for s in range(2 * NX)])


def shift_site(value, step):
    count = NZL * NY * NC
    return lax.ppermute(value, "site", [(i, (i + step) % count) for i in range(count)])


def site_index(z, y, c):
    return (z * NY + y) * NC + c


def shift_parts(value, dz, dy, dc):
    pairs = [
        (site_index(z, y, c), site_index((z + dz) % NZL, (y + dy) % NY, (c + dc) % NC))
        for z in range(NZL)
        for y in range(NY)
        for c in range(NC)
    ]
    return lax.ppermute(value, "site", pairs)


def sketch_kernel(count, order_ref, *refs):
    rows, probes_ref, outs = refs[:count], refs[count], refs[count + 1 :]
    step = pl.program_id(0)
    left = jnp.concatenate([r[...] for r in rows], axis=0)
    part = jnp.dot(left, probes_ref[...], preferred_element_type=F32)
    size = outs[0].shape[0]

    @pl.when(step == 0)
    def _():
        for d, out in enumerate(outs):
            out[...] = part[d * size : (d + 1) * size]

    @pl.when(step > 0)
    def _():
        for d, out in enumerate(outs):
            out[...] += part[d * size : (d + 1) * size]


def sketch_half(order, ensemble, probes, block, depth=1024):
    count = order.shape[0]
    width = probes.shape[1]
    steps = ensemble.shape[1] // depth
    specs = [
        pl.BlockSpec((block, depth), functools.partial(lambda b, k, o: (o[b], k), b))
        for b in range(count)
    ]
    specs.append(pl.BlockSpec((depth, width), lambda k, o: (k, 0)))
    out_rows = count * block // NX
    return pl.pallas_call(
        functools.partial(sketch_kernel, count),
        grid_spec=pltpu.PrefetchScalarGridSpec(
            num_scalar_prefetch=1,
            grid=(steps,),
            in_specs=specs,
            out_specs=[pl.BlockSpec((out_rows, width), lambda k, o: (0, 0))] * NX,
        ),
        out_shape=[jax.ShapeDtypeStruct((out_rows, width), F32)] * NX,
        compiler_params=params(),
        cost_estimate=cost(2 * count * block * probes.size, 2 * (count * block * ensemble.shape[1] + probes.size)),
    )(order, *([ensemble] * count), probes)


def gram_kernel(place_ref, own_ref, a_ref, b_ref, c_ref, z_ref, *refs):
    cuts, (send_ref, keep_ref, whole, packed) = refs[:NX], refs[NX:]
    s = own_ref[...] + a_ref[...] + b_ref[...] + c_ref[...] + z_ref[...]
    whole[...] = s
    width = 128
    for d, cut in enumerate(cuts):
        cut[...] = whole[:, pl.ds(pl.multiple_of(lax.rem(place_ref[3] + d, NX) * width, width), width)]
    for r in range(4):
        row = lax.dot_general(
            s[:, r * width : (r + 1) * width], s[:, r * width :], (((0,), (0,)), ((), ())),
            precision=FULL, preferred_element_type=F32,
        )
        for slot, (p, q) in enumerate(UPPER):
            if p == r:
                packed[slot * width : (slot + 1) * width, :] = row[:, (q - r) * width : (q - r + 1) * width]
    half = packed.shape[0] // 2
    core = place_ref[0]
    send_ref[...] = packed[pl.ds(pl.multiple_of((1 - core) * half, half), half), :]
    keep_ref[...] = packed[pl.ds(pl.multiple_of(core * half, half), half), :]


def gram_parts(place, *parts):
    rows, width = parts[0].shape
    half = len(UPPER) * 128 // 2
    out = pl.pallas_call(
        gram_kernel,
        in_specs=[SMEM] + [VMEM] * 5,
        out_specs=[VMEM] * (NX + 2),
        out_shape=[jax.ShapeDtypeStruct((rows, width // NX), F32)] * NX
        + [jax.ShapeDtypeStruct((half, 128), F32)] * 2,
        scratch_shapes=[pltpu.VMEM((rows, width), F32), pltpu.VMEM((2 * half, 128), F32)],
        compiler_params=params(),
        cost_estimate=cost(6 * rows * width * width, 8 * rows * width * 4),
    )(place, *parts)
    return out[:NX], out[NX], out[NX + 1]


def split_kernel(axis, ways, place_ref, *refs):
    ins, outs, total = refs[:-ways - 1], refs[-ways - 1 : -1], refs[-1]
    acc = ins[0][...]
    for r in ins[1:]:
        acc = acc + r[...]
    total[...] = acc
    rows = outs[0].shape[0]
    me = place_ref[axis]
    for d, out in enumerate(outs):
        out[...] = total[pl.ds(pl.multiple_of(lax.rem(me + d, ways) * rows, 8), rows), :]


def add_and_split(place, axis, ways, parts):
    rows, width = parts[0].shape
    return pl.pallas_call(
        functools.partial(split_kernel, axis, ways),
        in_specs=[SMEM] + [VMEM] * len(parts),
        out_specs=[VMEM] * ways,
        out_shape=[jax.ShapeDtypeStruct((rows // ways, width), F32)] * ways,
        scratch_shapes=[pltpu.VMEM((rows, width), F32)],
        compiler_params=params(),
        cost_estimate=cost(rows * width * 4, rows * width * 16),
    )(place, *parts)


def join_kernel(axis, ways, place_ref, *refs):
    ins, out = refs[:-1], refs[-1]
    rows = ins[0].shape[0]
    me = place_ref[axis]
    for d, r in enumerate(ins):
        out[pl.ds(pl.multiple_of(lax.rem(me - d + ways, ways) * rows, 8), rows), :] = r[...]


def join(place, axis, parts):
    rows, width = parts[0].shape
    ways = len(parts)
    return pl.pallas_call(
        functools.partial(join_kernel, axis, ways),
        in_specs=[SMEM] + [VMEM] * ways,
        out_specs=VMEM,
        out_shape=jax.ShapeDtypeStruct((rows * ways, width), F32),
        compiler_params=params(),
        cost_estimate=cost(0, rows * ways * width * 8),
    )(place, *parts)


def after(value, other):
    return lax.optimization_barrier((value, other))[0]


def exchange(move, pieces):
    return [pieces[0]] + [move(pieces[d], d) for d in range(1, len(pieces))]


def total_of(parts):
    out = parts[0]
    for p in parts[1:]:
        out = out + p
    return out


def shift_y(value, d):
    return shift_parts(value, 0, d, 0)


def shift_z(value, d):
    return shift_parts(value, d, 0, 0)


def swap_core(value):
    return shift_parts(value, 0, 0, 1)


def split_halves_kernel(place_ref, mine_ref, theirs_ref, *refs):
    outs, whole = refs[:-1], refs[-1]
    rows = mine_ref.shape[0]
    half = place_ref[4]
    whole[pl.ds(pl.multiple_of(half * rows, 8), rows), :] = mine_ref[...]
    whole[pl.ds(pl.multiple_of((1 - half) * rows, 8), rows), :] = theirs_ref[...]
    size = outs[0].shape[0]
    for d, out in enumerate(outs):
        out[...] = whole[pl.ds(pl.multiple_of(lax.rem(place_ref[2] + d, NZL) * size, 8), size), :]


def split_halves(place, mine, theirs):
    rows, width = mine.shape
    return pl.pallas_call(
        split_halves_kernel,
        in_specs=[SMEM, VMEM, VMEM],
        out_specs=[VMEM] * NZL,
        out_shape=[jax.ShapeDtypeStruct((2 * rows // NZL, width), F32)] * NZL,
        scratch_shapes=[pltpu.VMEM((2 * rows, width), F32)],
        compiler_params=params(),
        cost_estimate=cost(0, 16 * rows * width),
    )(place, mine, theirs)


def repack_y_kernel(place_ref, *refs):
    ins, outs = refs[:NZL], refs[NZL:]
    rows = ins[0].shape[0] // NY
    for d, out in enumerate(outs):
        at = pl.ds(pl.multiple_of(lax.rem(place_ref[1] + d, NY) * rows, 8), rows)
        for z, r in enumerate(ins):
            out[z * rows : (z + 1) * rows, :] = r[at, :]


def repack_y(place, parts):
    shape = jax.ShapeDtypeStruct(parts[0].shape, F32)
    size = parts[0].size
    return pl.pallas_call(
        repack_y_kernel,
        in_specs=[SMEM] + [VMEM] * NZL,
        out_specs=[VMEM] * NY,
        out_shape=[shape] * NY,
        compiler_params=params(),
        cost_estimate=cost(0, 32 * size),
    )(place, *parts)


def repack_core_kernel(block, place_ref, *refs):
    ins, (keep, send) = refs[:NY], refs[NY:]
    core = place_ref[0]
    pieces = ins[0].shape[0] // (NC * block)
    for y, r in enumerate(ins):
        for z in range(pieces):
            row = (y * pieces + z) * block
            keep[row : row + block, :] = r[pl.ds(pl.multiple_of((z * NC + core) * block, 8), block), :]
            send[row : row + block, :] = r[pl.ds(pl.multiple_of((z * NC + 1 - core) * block, 8), block), :]


def repack_core(place, parts, block):
    rows, width = parts[0].shape
    shape = jax.ShapeDtypeStruct((rows * NY // NC, width), F32)
    return pl.pallas_call(
        functools.partial(repack_core_kernel, block),
        in_specs=[SMEM] + [VMEM] * NY,
        out_specs=[VMEM] * 2,
        out_shape=[shape] * 2,
        compiler_params=params(),
        cost_estimate=cost(0, 32 * rows * width),
    )(place, *parts)


def block_inverse(tile_rows, size, lane):
    rows = list(tile_rows)
    done = [[] for _ in rows]
    sub = lax.broadcasted_iota(jnp.int32, (8, size), 0)
    for j in range(0, size, 4):
        q, o = divmod(j, 8)
        in_block = (lane >= j) & (lane < j + 4)
        base = rows[q]
        spread = [jnp.broadcast_to(base[o + a : o + a + 1, :], (8, size)) for a in range(4)]
        s = [
            [jnp.broadcast_to(spread[a][:, j + b : j + b + 1], (8, size)) if b >= a else None for b in range(4)]
            for a in range(4)
        ]
        up = [jnp.where(in_block, jnp.where(lane == j + a, 1.0, 0.0), spread[a]) for a in range(4)]
        mult = [[None] * 4 for _ in range(4)]
        root, recip = [], []
        for a in range(4):
            root.append(lax.rsqrt(s[a][a]))
            recip.append(root[a] * root[a])
            for b in range(a + 1, 4):
                mult[b][a] = s[a][b] * recip[a]
                for c in range(b, 4):
                    s[b][c] = s[b][c] - mult[b][a] * s[a][c]
                up[b] = up[b] - mult[b][a] * up[a]
        v = [None] * 4
        for a in range(3, -1, -1):
            v[a] = recip[a] * up[a]
            for b in range(a + 1, 4):
                v[a] = v[a] - mult[b][a] * v[b]
        for t in range(q + (1 if o == 4 else 0), len(rows)):
            cur = rows[t]
            new = jnp.where(in_block, 0.0, cur)
            for a in range(4):
                new = new - jnp.broadcast_to(cur[:, j + a : j + a + 1], (8, size)) * v[a]
            rows[t] = jnp.where(sub >= o + 4, new, cur) if t == q else new
        for a in range(4):
            done[q].append(root[a] * up[a])
    out = []
    for q, parts in enumerate(done):
        whole = parts[0]
        for a in range(1, 8):
            whole = jnp.where(sub == a, parts[a], whole)
        out.append(jnp.where(lane <= sub + 8 * q, whole, 0.0))
    return out


def factor_steps(x_ref, first, last):
    width = 128
    n = x_ref.shape[0]
    steps = n // width
    lane = lax.broadcasted_iota(jnp.int32, (8, width), 1)
    for k in range(first, last):
        lo, hi = k * width, (k + 1) * width
        tiles = [x_ref[lo + 8 * t : lo + 8 * t + 8, lo:hi] for t in range(width // 8)]
        inv = jnp.concatenate(block_inverse(tiles, width, lane), axis=0)
        if k > 0:
            x_ref[lo:hi, :lo] = jnp.dot(inv, x_ref[lo:hi, :lo], precision=FULL, preferred_element_type=F32)
        x_ref[lo:hi, lo:hi] = inv
        if k < steps - 1:
            upper = jnp.dot(inv, x_ref[lo:hi, hi:], precision=FULL, preferred_element_type=F32)
            x_ref[lo:hi, hi:] = upper
            x_ref[hi:, lo:hi] = jnp.zeros((n - hi, width), F32)
            x_ref[hi:, :] -= lax.dot_general(
                upper, x_ref[lo:hi, :], (((0,), (0,)), ((), ())), precision=FULL, preferred_element_type=F32
            )
            x_ref[lo:hi, hi:] = jnp.zeros((width, n - hi), F32)


def factor_open_kernel(last, place_ref, half_ref, other_ref, x_ref, packed):
    width = 128
    n = x_ref.shape[0]
    half = half_ref.shape[0]
    core = place_ref[0]
    packed[pl.ds(pl.multiple_of(core * half, half), half), :] = half_ref[...]
    packed[pl.ds(pl.multiple_of((1 - core) * half, half), half), :] = other_ref[...]
    x_ref[...] = jnp.zeros((n, n), F32)
    for slot, (p, q) in enumerate(UPPER):
        x_ref[p * width : (p + 1) * width, q * width : (q + 1) * width] = packed[slot * width : (slot + 1) * width, :]
    factor_steps(x_ref, 0, last)


def factor_open(place, half, other, n, last):
    return pl.pallas_call(
        functools.partial(factor_open_kernel, last),
        in_specs=[SMEM, VMEM, VMEM],
        out_specs=VMEM,
        out_shape=jax.ShapeDtypeStruct((n, n), F32),
        scratch_shapes=[pltpu.VMEM((2 * half.shape[0], 128), F32)],
        compiler_params=params(),
        cost_estimate=cost(10 * last * n * n * n, 8 * n * n),
    )(place, half, other)


def factor_more_kernel(first, last, in_ref, x_ref):
    x_ref[...] = in_ref[...]
    factor_steps(x_ref, first, last)


def factor_more(value, first, last):
    n = value.shape[0]
    return pl.pallas_call(
        functools.partial(factor_more_kernel, first, last),
        in_specs=[VMEM],
        out_specs=VMEM,
        out_shape=jax.ShapeDtypeStruct((n, n), F32),
        compiler_params=params(),
        cost_estimate=cost(10 * (last - first) * n * n * n, 8 * n * n),
    )(value)


def lines_kernel(group, block, where_ref, low_ref, own_ref, high_ref, *refs):
    factors, outs, top, rest = refs[:NX], refs[NX : 2 * NX], refs[-2], refs[-1]
    rows = own_ref.shape[0]
    for at, table in enumerate((low_ref, own_ref, high_ref)):
        value = table[...]
        first = value.astype(jnp.bfloat16)
        top[at * rows : (at + 1) * rows, :] = first
        rest[at * rows : (at + 1) * rows, :] = (value - first.astype(F32)).astype(jnp.bfloat16)
    lines, span = factors[0].shape
    links = span // block
    groups = lines // group
    for d in range(NX):

        def one(g, carry, d=d):
            at = [
                pl.multiple_of(where_ref[(d * groups + g) * links + t] * block, block) for t in range(links)
            ]
            line = pl.ds(pl.multiple_of(g * group, group), group)
            f = factors[d][line, :].astype(jnp.bfloat16)
            first = jnp.concatenate([top[pl.ds(a, block), :] for a in at], axis=0)
            second = jnp.concatenate([rest[pl.ds(a, block), :] for a in at], axis=0)
            outs[d][line, :] = jnp.dot(f, first, preferred_element_type=F32) + jnp.dot(
                f, second, preferred_element_type=F32
            )
            return carry

        lax.fori_loop(0, groups, one, 0, unroll=True)


def lines_part(where, low, own, high, factors, group, block):
    rows, width = own.shape
    lines = factors[0].shape[0]
    return pl.pallas_call(
        functools.partial(lines_kernel, group, block),
        in_specs=[SMEM] + [VMEM] * (3 + NX),
        out_specs=[VMEM] * NX,
        out_shape=[jax.ShapeDtypeStruct((lines, width), F32)] * NX,
        scratch_shapes=[pltpu.VMEM((3 * rows, width), jnp.bfloat16)] * 2,
        compiler_params=params(),
        cost_estimate=cost(64 * lines * width * NX * 256, 3 * rows * width * 4),
    )(where, low, own, high, *factors)


def finish_kernel(scale, place_ref, *refs):
    ins, x_ref, out_ref, wide = refs[:NX], refs[NX], refs[NX + 1], refs[NX + 2]
    width = ins[0].shape[1]
    me = place_ref[3]
    for d, r in enumerate(ins):
        wide[:, pl.ds(pl.multiple_of(lax.rem(me + d, NX) * width, width), width)] = r[...]
    out_ref[...] = scale * lax.dot_general(
        wide[...], x_ref[...], (((1,), (1,)), ((), ())), precision=FULL, preferred_element_type=F32
    )


def finish(place, parts, inverse, scale):
    lines = parts[0].shape[0]
    n = inverse.shape[0]
    return pl.pallas_call(
        functools.partial(finish_kernel, scale),
        in_specs=[SMEM] + [VMEM] * (NX + 1),
        out_specs=VMEM,
        out_shape=jax.ShapeDtypeStruct((lines, n), F32),
        scratch_shapes=[pltpu.VMEM((lines, n), F32)],
        compiler_params=params(),
        cost_estimate=cost(12 * lines * n * n, 8 * n * n),
    )(place, *parts, inverse)


def per_device(ensemble, probes, site_bus, incidence, shift_factors):
    sites = lax.axis_size("site")
    samps = lax.axis_size("samp")
    site = lax.axis_index("site")
    samp = lax.axis_index("samp")
    site_rows = ensemble.shape[0]
    n = probes.shape[1]
    block = site_rows // sites
    per = sites // samps
    half, x = samp // NX, samp % NX
    place = jnp.stack([site % NC, site // NC % NY, site // (NC * NY), x, half]).astype(jnp.int32)

    lines, span = shift_factors.shape
    groups, links = incidence.shape
    lists = jnp.pad(incidence.astype(F32), ((0, 0), (0, span - links)))
    carried = jnp.concatenate([shift_factors.astype(F32), lists], axis=0)
    carried = [carried] + [shift_x(carried, d) for d in range(1, NX)]
    factors = [c[:lines] for c in carried]
    wanted = jnp.stack([c[lines:, :links] for c in carried]).astype(jnp.int32).reshape(-1)

    table = site_bus.reshape(sites, sites)
    owners = lax.dynamic_index_in_dim(table, site, 0, keepdims=False) // sites
    slot = jnp.arange(sites, dtype=jnp.int32)
    block_for = jnp.sum(jnp.where(owners[None, :] == slot[:, None], slot[None, :], 0), axis=1)
    came_from = jnp.arange(sites * sites, dtype=jnp.int32) // sites
    source = jnp.sum(jnp.where(site_bus[None, :] == wanted[:, None], came_from[None, :], 0), axis=1)
    owner = wanted // sites
    dz = (owner // (NC * NY) - source // (NC * NY)) % NZL
    dy = (owner // NC - source // NC) % NY
    dc = (owner - source) % NC
    where = jnp.remainder(owner - site + 1, sites) * sites + (dc * NY + dy) * NZL + dz

    def order_for(h):
        devices = h * NX + (x + jnp.arange(NX, dtype=jnp.int32)) % NX
        want = (devices[:, None] * per + jnp.arange(per, dtype=jnp.int32)[None, :]).reshape(-1)
        return jnp.sum(jnp.where(want[:, None] == slot[None, :], block_for[None, :], 0), axis=1)

    away = sketch_half(order_for(1 - half), ensemble, probes, block)
    home = sketch_half(order_for(half), ensemble, probes, block)
    sent = away[0]
    for d in range(1, NX):
        sent = sent + shift_x(away[d], d)
    crossed = swap_half(sent)
    around = [shift_x(home[d], d) for d in range(1, NX)]
    cuts, send, keep = gram_parts(place, home[0], *around, crossed)

    got = swap_core(send)
    pieces = add_and_split(place, 1, NY, [keep, got])
    part = total_of(exchange(shift_y, pieces))
    cuts = exchange(shift_x, [after(c, part) for c in cuts])
    part = total_of([part] + [shift_z(part, d) for d in range(1, NZL)])
    part = part + swap_half(part)
    column = join(place, 3, [after(c, part) for c in cuts])
    crossing = swap_half(column)
    part = total_of([part] + [shift_x(part, d) for d in range(1, NX)])
    run = join(place, 1, [part] + [shift_y(part, d) for d in range(1, NY)])
    other = swap_core(run)
    blocks = exchange(shift_z, split_halves(place, column, after(crossing, other)))
    inverse = factor_open(place, run, other, n, 1)
    blocks = exchange(shift_y, repack_y(place, [after(b, inverse) for b in blocks]))
    inverse = factor_more(inverse, 1, 2)
    kept, sent = repack_core(place, [after(b, inverse) for b in blocks], block)
    own = jnp.concatenate([kept, swap_core(sent)], axis=0)
    low = shift_site(own, 1)
    high = shift_site(own, -1)
    inverse = factor_more(inverse, 2, 3)
    inverse = factor_more(inverse, 3, 4)
    parts = lines_part(where, low, own, high, factors, lines // groups, block)
    parts = [parts[0]] + [shift_x(parts[d], -d) for d in range(1, NX)]
    return finish(place, parts, inverse, math.sqrt(site_rows * sites))


def solution(mesh):
    in_specs = (
        P("site", "samp"),
        P("samp", None),
        P(),
        P(("samp", "site"), None),
        P(("samp", "site"), None),
    )
    return jax.shard_map(
        per_device, mesh=mesh, in_specs=in_specs, out_specs=P(("samp", "site"), None), check_vma=False
    )
```

```python
import functools
import math

import jax
import jax.numpy as jnp
from jax import lax
from jax.experimental import pallas as pl
from jax.experimental.pallas import tpu as pltpu
from jax.sharding import PartitionSpec as P

FULL = lax.Precision.HIGHEST
F32 = jnp.float32
NX = 4
NZL = 4
NY = 4
NC = 2
UPPER = ((0, 0), (0, 1), (0, 2), (0, 3), (3, 3), (1, 1), (1, 2), (1, 3), (2, 2), (2, 3))
VMEM = pl.BlockSpec(memory_space=pltpu.VMEM)
SMEM = pl.BlockSpec(memory_space=pltpu.SMEM)


def params(mib=48):
    return pltpu.CompilerParams(vmem_limit_bytes=mib * 1024 * 1024)


def cost(flops, moved):
    return pl.CostEstimate(flops=flops, bytes_accessed=moved, transcendentals=0)


def shift_x(value, step):
    pairs = [(h * NX + x, h * NX + (x + step) % NX) for h in range(2) for x in range(NX)]
    return lax.ppermute(value, "samp", pairs)


def swap_half(value):
    return lax.ppermute(value, "samp", [(s, (s + NX) % (2 * NX)) for s in range(2 * NX)])


def site_index(z, y, c):
    return (z * NY + y) * NC + c


def shift_parts(value, dz, dy, dc):
    pairs = [
        (site_index(z, y, c), site_index((z + dz) % NZL, (y + dy) % NY, (c + dc) % NC))
        for z in range(NZL)
        for y in range(NY)
        for c in range(NC)
    ]
    return lax.ppermute(value, "site", pairs)


def sketch_kernel(count, order_ref, *refs):
    rows, probes_ref, outs = refs[:count], refs[count], refs[count + 1 :]
    step = pl.program_id(0)
    left = jnp.concatenate([r[...] for r in rows], axis=0)
    part = jnp.dot(left, probes_ref[...], preferred_element_type=F32)
    size = outs[0].shape[0]

    @pl.when(step == 0)
    def _():
        for d, out in enumerate(outs):
            out[...] = part[d * size : (d + 1) * size]

    @pl.when(step > 0)
    def _():
        for d, out in enumerate(outs):
            out[...] += part[d * size : (d + 1) * size]


def sketch_half(order, ensemble, probes, block, mib, depth=2048):
    count = order.shape[0]
    width = probes.shape[1]
    steps = ensemble.shape[1] // depth
    specs = [
        pl.BlockSpec((block, depth), functools.partial(lambda b, k, o: (o[b], k), b))
        for b in range(count)
    ]
    specs.append(pl.BlockSpec((depth, width), lambda k, o: (k, 0)))
    out_rows = count * block // NX
    return pl.pallas_call(
        functools.partial(sketch_kernel, count),
        grid_spec=pltpu.PrefetchScalarGridSpec(
            num_scalar_prefetch=1,
            grid=(steps,),
            in_specs=specs,
            out_specs=[pl.BlockSpec((out_rows, width), lambda k, o: (0, 0))] * NX,
        ),
        out_shape=[jax.ShapeDtypeStruct((out_rows, width), F32)] * NX,
        compiler_params=params(mib),
        cost_estimate=cost(2 * count * block * probes.size, 2 * (count * block * ensemble.shape[1] + probes.size)),
    )(order, *([ensemble] * count), probes)


def gram_kernel(place_ref, own_ref, a_ref, b_ref, c_ref, z_ref, *refs):
    cuts, (send_ref, keep_ref, whole, packed) = refs[:NX], refs[NX:]
    s = own_ref[...] + a_ref[...] + b_ref[...] + c_ref[...] + z_ref[...]
    whole[...] = s
    width = 128
    for d, cut in enumerate(cuts):
        cut[...] = whole[:, pl.ds(pl.multiple_of(lax.rem(place_ref[3] + d, NX) * width, width), width)]
    for r in range(4):
        row = lax.dot_general(
            s[:, r * width : (r + 1) * width], s[:, r * width :], (((0,), (0,)), ((), ())),
            precision=FULL, preferred_element_type=F32,
        )
        for slot, (p, q) in enumerate(UPPER):
            if p == r:
                packed[slot * width : (slot + 1) * width, :] = row[:, (q - r) * width : (q - r + 1) * width]
    half = packed.shape[0] // 2
    core = place_ref[0]
    send_ref[...] = packed[pl.ds(pl.multiple_of((1 - core) * half, half), half), :]
    keep_ref[...] = packed[pl.ds(pl.multiple_of(core * half, half), half), :]


def gram_parts(place, *parts):
    rows, width = parts[0].shape
    half = len(UPPER) * 128 // 2
    out = pl.pallas_call(
        gram_kernel,
        in_specs=[SMEM] + [VMEM] * 5,
        out_specs=[VMEM] * (NX + 2),
        out_shape=[jax.ShapeDtypeStruct((rows, width // NX), F32)] * NX
        + [jax.ShapeDtypeStruct((half, 128), F32)] * 2,
        scratch_shapes=[pltpu.VMEM((rows, width), F32), pltpu.VMEM((2 * half, 128), F32)],
        compiler_params=params(),
        cost_estimate=cost(6 * rows * width * width, 8 * rows * width * 4),
    )(place, *parts)
    return out[:NX], out[NX], out[NX + 1]


def split_kernel(axis, ways, place_ref, *refs):
    ins, outs, total = refs[:-ways - 1], refs[-ways - 1 : -1], refs[-1]
    acc = ins[0][...]
    for r in ins[1:]:
        acc = acc + r[...]
    total[...] = acc
    rows = outs[0].shape[0]
    me = place_ref[axis]
    for d, out in enumerate(outs):
        out[...] = total[pl.ds(pl.multiple_of(lax.rem(me + d, ways) * rows, 8), rows), :]


def add_and_split(place, axis, ways, parts):
    rows, width = parts[0].shape
    return pl.pallas_call(
        functools.partial(split_kernel, axis, ways),
        in_specs=[SMEM] + [VMEM] * len(parts),
        out_specs=[VMEM] * ways,
        out_shape=[jax.ShapeDtypeStruct((rows // ways, width), F32)] * ways,
        scratch_shapes=[pltpu.VMEM((rows, width), F32)],
        compiler_params=params(),
        cost_estimate=cost(rows * width * 4, rows * width * 16),
    )(place, *parts)


def join_kernel(axis, ways, place_ref, *refs):
    ins, out = refs[:-1], refs[-1]
    rows = ins[0].shape[0]
    me = place_ref[axis]
    for d, r in enumerate(ins):
        out[pl.ds(pl.multiple_of(lax.rem(me - d + ways, ways) * rows, 8), rows), :] = r[...]


def join(place, axis, parts):
    rows, width = parts[0].shape
    ways = len(parts)
    return pl.pallas_call(
        functools.partial(join_kernel, axis, ways),
        in_specs=[SMEM] + [VMEM] * ways,
        out_specs=VMEM,
        out_shape=jax.ShapeDtypeStruct((rows * ways, width), F32),
        compiler_params=params(),
        cost_estimate=cost(0, rows * ways * width * 8),
    )(place, *parts)


def after(value, other):
    return lax.optimization_barrier((value, other))[0]


def exchange(move, pieces):
    return [pieces[0]] + [move(pieces[d], d) for d in range(1, len(pieces))]


def total_of(parts):
    out = parts[0]
    for p in parts[1:]:
        out = out + p
    return out


def shift_y(value, d):
    return shift_parts(value, 0, d, 0)


def shift_z(value, d):
    return shift_parts(value, d, 0, 0)


def swap_core(value):
    return shift_parts(value, 0, 0, 1)


def turn_y_kernel(place_ref, *refs):
    ins, outs, whole = refs[:NX], refs[NX:-1], refs[-1]
    rows = ins[0].shape[0]
    for d, r in enumerate(ins):
        whole[pl.ds(pl.multiple_of(lax.rem(place_ref[3] - d + NX, NX) * rows, 8), rows), :] = r[...]
    size = outs[0].shape[0] // 2
    for d, out in enumerate(outs):
        at = lax.rem(place_ref[1] + d, NY) * size
        for z in range(2):
            out[z * size : (z + 1) * size, :] = whole[pl.ds(pl.multiple_of(z * 2 * rows + at, 8), size), :]


def turn_z_kernel(place_ref, mine_ref, theirs_ref, *refs):
    outs, whole = refs[:-1], refs[-1]
    rows = mine_ref.shape[0]
    half = place_ref[4]
    whole[pl.ds(pl.multiple_of(half * rows, 8), rows), :] = mine_ref[...]
    whole[pl.ds(pl.multiple_of((1 - half) * rows, 8), rows), :] = theirs_ref[...]
    size = rows // (2 * NY)
    for d, out in enumerate(outs):
        to = lax.rem(place_ref[2] + d, NZL)
        at = to // 2 * rows + to % 2 * size
        for y in range(NY):
            out[y * size : (y + 1) * size, :] = whole[pl.ds(pl.multiple_of(at + y * 2 * size, 8), size), :]


def turn_core_kernel(block, place_ref, *refs):
    ins, (keep, pair) = refs[:NZL], refs[NZL:]
    core = place_ref[0]
    count = ins[0].shape[0] // (NC * block)
    for z, r in enumerate(ins):
        for y in range(count):
            row = (z * count + y) * block
            keep[row : row + block, :] = r[pl.ds(pl.multiple_of((y * NC + core) * block, 8), block), :]
            pair[row : row + block, :] = r[pl.ds(pl.multiple_of((y * NC + 1 - core) * block, 8), block), :]


def turn(kernel, place, parts, shapes, scratch_rows=0):
    width = parts[0].shape[1]
    moved = 8 * sum(p.size for p in parts)
    return pl.pallas_call(
        kernel,
        in_specs=[SMEM] + [VMEM] * len(parts),
        out_specs=[VMEM] * len(shapes),
        out_shape=[jax.ShapeDtypeStruct((r, width), F32) for r in shapes],
        scratch_shapes=[pltpu.VMEM((scratch_rows, width), F32)] if scratch_rows else [],
        compiler_params=params(),
        cost_estimate=cost(0, moved),
    )(place, *parts)


def cross_chip(value, same_core):
    chips = NZL * NY
    pairs = []
    for p in range(chips):
        up, down = (p + 1) % chips * NC, (p - 1) % chips * NC + 1
        pairs += [(p * NC, up), (p * NC + 1, down)] if same_core else [(p * NC + 1, up), (p * NC, down)]
    return lax.ppermute(value, "site", pairs)


def block_inverse(tile_rows, size, lane):
    rows = list(tile_rows)
    done = [[] for _ in rows]
    sub = lax.broadcasted_iota(jnp.int32, (8, size), 0)

    def wide(v, at):
        return jnp.broadcast_to(v[:, at : at + 1], (8, size))

    def tall(j):
        q, o = divmod(j, 8)
        return [jnp.broadcast_to(rows[q][o + a : o + a + 1, :], (8, size)) for a in range(4)]

    spread = tall(0)
    s = [[wide(spread[a], b) if b >= a else None for b in range(4)] for a in range(4)]
    for j in range(0, size, 4):
        q, o = divmod(j, 8)
        in_block = (lane >= j) & (lane < j + 4)
        up = [jnp.where(in_block, jnp.where(lane == j + a, 1.0, 0.0), spread[a]) for a in range(4)]
        a, b, c = s[0][0], s[0][1], s[1][1]
        e, f, g, h = s[0][2], s[1][2], s[0][3], s[1][3]
        inv1 = 1.0 / (a * c - b * b)
        n20, n21 = e * c - f * b, f * a - e * b
        n30, n31 = g * c - h * b, h * a - g * b
        s22 = s[2][2] - inv1 * (n20 * e + n21 * f)
        s23 = s[2][3] - inv1 * (n20 * g + n21 * h)
        s33 = s[3][3] - inv1 * (n30 * g + n31 * h)
        w20, w21, w30, w31 = n20 * inv1, n21 * inv1, n30 * inv1, n31 * inv1
        ca, cb, cc = c * inv1, b * inv1, a * inv1
        inv2 = 1.0 / (s22 * s33 - s23 * s23)

        def solve(t0, t1, t2, t3):
            u2 = t2 - (w20 * t0 + w21 * t1)
            u3 = t3 - (w30 * t0 + w31 * t1)
            v2 = inv2 * (s33 * u2 - s23 * u3)
            v3 = inv2 * (s22 * u3 - s23 * u2)
            v0 = (ca * t0 - cb * t1) - (w20 * v2 + w30 * v3)
            v1 = (cc * t1 - cb * t0) - (w21 * v2 + w31 * v3)
            return v0, v1, v2, v3

        v = solve(*up)
        more = j + 4 < size
        if more:
            cross = [[wide(spread[k], j + 4 + m) for m in range(4)] for k in range(4)]
            coming = tall(j + 4)
            nexts = [[None] * 4 for _ in range(4)]
            for m in range(4):
                vm = solve(cross[0][m], cross[1][m], cross[2][m], cross[3][m])
                for l in range(m + 1):
                    nexts[l][m] = wide(coming[l], j + 4 + m) - (
                        (cross[0][l] * vm[0] + cross[1][l] * vm[1]) + (cross[2][l] * vm[2] + cross[3][l] * vm[3])
                    )
            ahead = [
                jnp.where(in_block, 0.0, coming[m])
                - ((cross[0][m] * v[0] + cross[1][m] * v[1]) + (cross[2][m] * v[2] + cross[3][m] * v[3]))
                for m in range(4)
            ]
        for t in range(q + (1 if o == 4 else 0), len(rows)):
            cur = rows[t]
            new = jnp.where(in_block, 0.0, cur) - (
                (wide(cur, j) * v[0] + wide(cur, j + 1) * v[1]) + (wide(cur, j + 2) * v[2] + wide(cur, j + 3) * v[3])
            )
            rows[t] = jnp.where(sub >= o + 4, new, cur) if t == q else new
        r0 = lax.rsqrt(a)
        m1 = b * (r0 * r0)
        r1 = lax.rsqrt(c - m1 * b)
        r2 = lax.rsqrt(s22)
        m3 = s23 * (r2 * r2)
        r3 = lax.rsqrt(s33 - m3 * s23)
        u2 = up[2] - (w20 * up[0] + w21 * up[1])
        u3 = up[3] - (w30 * up[0] + w31 * up[1])
        done[q] += [r0 * up[0], r1 * (up[1] - m1 * up[0]), r2 * u2, r3 * (u3 - m3 * u2)]
        if more:
            spread, s = ahead, nexts
    out = []
    for q, parts in enumerate(done):
        whole = parts[0]
        for k in range(1, 8):
            whole = jnp.where(sub == k, parts[k], whole)
        out.append(jnp.where(lane <= sub + 8 * q, whole, 0.0))
    return out


def factor_steps(x_ref, first, last):
    width = 128
    n = x_ref.shape[0]
    steps = n // width
    lane = lax.broadcasted_iota(jnp.int32, (8, width), 1)
    for k in range(first, last):
        lo, hi = k * width, (k + 1) * width
        tiles = [x_ref[lo + 8 * t : lo + 8 * t + 8, lo:hi] for t in range(width // 8)]
        inv = jnp.concatenate(block_inverse(tiles, width, lane), axis=0)
        if k > 0:
            x_ref[lo:hi, :lo] = jnp.dot(inv, x_ref[lo:hi, :lo], precision=FULL, preferred_element_type=F32)
        x_ref[lo:hi, lo:hi] = inv
        if k < steps - 1:
            upper = jnp.dot(inv, x_ref[lo:hi, hi:], precision=FULL, preferred_element_type=F32)
            x_ref[lo:hi, hi:] = upper
            x_ref[hi:, lo:hi] = jnp.zeros((n - hi, width), F32)
            x_ref[hi:, :] -= lax.dot_general(
                upper, x_ref[lo:hi, :], (((0,), (0,)), ((), ())), precision=FULL, preferred_element_type=F32
            )
            x_ref[lo:hi, hi:] = jnp.zeros((width, n - hi), F32)


def factor_open_kernel(last, place_ref, half_ref, other_ref, x_ref, scale_ref, packed):
    width = 128
    n = x_ref.shape[0]
    half = half_ref.shape[0]
    core = place_ref[0]
    packed[pl.ds(pl.multiple_of(core * half, half), half), :] = half_ref[...]
    packed[pl.ds(pl.multiple_of((1 - core) * half, half), half), :] = other_ref[...]
    x_ref[...] = jnp.zeros((n, n), F32)
    eye = lax.broadcasted_iota(jnp.int32, (width, width), 0) == lax.broadcasted_iota(jnp.int32, (width, width), 1)
    across, down = [], []
    for k in range(n // width):
        slot = UPPER.index((k, k))
        diag = jnp.where(eye, packed[slot * width : (slot + 1) * width, :], 0.0)
        across.append(lax.rsqrt(jnp.sum(diag, axis=0, keepdims=True)))
        down.append(lax.rsqrt(jnp.sum(diag, axis=1, keepdims=True)))
        scale_ref[:, k * width : (k + 1) * width] = jnp.broadcast_to(across[k], (8, width))
    for slot, (p, q) in enumerate(UPPER):
        x_ref[p * width : (p + 1) * width, q * width : (q + 1) * width] = (
            packed[slot * width : (slot + 1) * width, :] * down[p] * across[q]
        )
    factor_steps(x_ref, 0, last)


def factor_open(place, half, other, n, last):
    return pl.pallas_call(
        functools.partial(factor_open_kernel, last),
        in_specs=[SMEM, VMEM, VMEM],
        out_specs=[VMEM] * 2,
        out_shape=[jax.ShapeDtypeStruct((n, n), F32), jax.ShapeDtypeStruct((8, n), F32)],
        scratch_shapes=[pltpu.VMEM((2 * half.shape[0], 128), F32)],
        compiler_params=params(),
        cost_estimate=cost(10 * last * n * n * n, 8 * n * n),
    )(place, half, other)


def factor_more_kernel(first, last, in_ref, x_ref):
    x_ref[...] = in_ref[...]
    factor_steps(x_ref, first, last)


def factor_more(value, first, last):
    n = value.shape[0]
    return pl.pallas_call(
        functools.partial(factor_more_kernel, first, last),
        in_specs=[VMEM],
        out_specs=VMEM,
        out_shape=jax.ShapeDtypeStruct((n, n), F32),
        compiler_params=params(),
        cost_estimate=cost(10 * (last - first) * n * n * n, 8 * n * n),
    )(value)


def lines_kernel(count, group, block, where_ref, *refs):
    tables, refs = refs[:count], refs[count:]
    factors, outs, top, rest = refs[:NX], refs[NX : 2 * NX], refs[-2], refs[-1]
    rows = tables[0].shape[0]
    for at, table in enumerate(tables):
        value = table[...]
        first = value.astype(jnp.bfloat16)
        top[at * rows : (at + 1) * rows, :] = first
        rest[at * rows : (at + 1) * rows, :] = (value - first.astype(F32)).astype(jnp.bfloat16)
    lines, span = factors[0].shape
    links = span // block
    groups = lines // group
    for d in range(NX):

        def one(g, carry, d=d):
            at = [
                pl.multiple_of(where_ref[(d * groups + g) * links + t] * block, block) for t in range(links)
            ]
            line = pl.ds(pl.multiple_of(g * group, group), group)
            f = factors[d][line, :].astype(jnp.bfloat16)
            first = jnp.concatenate([top[pl.ds(a, block), :] for a in at], axis=0)
            second = jnp.concatenate([rest[pl.ds(a, block), :] for a in at], axis=0)
            outs[d][line, :] = jnp.dot(f, first, preferred_element_type=F32) + jnp.dot(
                f, second, preferred_element_type=F32
            )
            return carry

        lax.fori_loop(0, groups, one, 0, unroll=True)


def lines_part(where, tables, factors, group, block):
    rows, width = tables[0].shape
    lines = factors[0].shape[0]
    return pl.pallas_call(
        functools.partial(lines_kernel, len(tables), group, block),
        in_specs=[SMEM] + [VMEM] * (len(tables) + NX),
        out_specs=[VMEM] * NX,
        out_shape=[jax.ShapeDtypeStruct((lines, width), F32)] * NX,
        scratch_shapes=[pltpu.VMEM((len(tables) * rows, width), jnp.bfloat16)] * 2,
        compiler_params=params(),
        cost_estimate=cost(64 * lines * width * NX * 256, 4 * len(tables) * rows * width),
    )(where, *tables, *factors)


def finish_kernel(scale, place_ref, *refs):
    ins, (x_ref, unit_ref, out_ref, wide) = refs[:NX], refs[NX:]
    width = ins[0].shape[1]
    me = place_ref[3]
    for d, r in enumerate(ins):
        wide[:, pl.ds(pl.multiple_of(lax.rem(me + d, NX) * width, width), width)] = r[...]
    out_ref[...] = lax.dot_general(
        wide[...] * (scale * unit_ref[0:1, :]), x_ref[...], (((1,), (1,)), ((), ())), precision=FULL, preferred_element_type=F32
    )


def finish(place, parts, inverse, unit, scale):
    lines = parts[0].shape[0]
    n = inverse.shape[0]
    return pl.pallas_call(
        functools.partial(finish_kernel, scale),
        in_specs=[SMEM] + [VMEM] * (NX + 2),
        out_specs=VMEM,
        out_shape=jax.ShapeDtypeStruct((lines, n), F32),
        scratch_shapes=[pltpu.VMEM((lines, n), F32)],
        compiler_params=params(),
        cost_estimate=cost(12 * lines * n * n, 8 * n * n),
    )(place, *parts, inverse, unit)


def per_device(ensemble, probes, site_bus, incidence, shift_factors):
    sites = lax.axis_size("site")
    samps = lax.axis_size("samp")
    site = lax.axis_index("site")
    samp = lax.axis_index("samp")
    site_rows = ensemble.shape[0]
    n = probes.shape[1]
    block = site_rows // sites
    per = sites // samps
    half, x = samp // NX, samp % NX
    place = jnp.stack([site % NC, site // NC % NY, site // (NC * NY), x, half]).astype(jnp.int32)

    lines, span = shift_factors.shape
    groups, links = incidence.shape
    lists = jnp.pad(incidence.astype(F32), ((0, 0), (0, span - links)))
    carried = jnp.concatenate([shift_factors.astype(F32), lists], axis=0)
    carried = [carried] + [shift_x(carried, d) for d in range(1, NX)]
    factors = [c[:lines] for c in carried]
    wanted = jnp.stack([c[lines:, :links] for c in carried]).astype(jnp.int32).reshape(-1)

    table = site_bus.reshape(sites, sites)
    owners = lax.dynamic_index_in_dim(table, site, 0, keepdims=False) // sites
    slot = jnp.arange(sites, dtype=jnp.int32)
    block_for = jnp.sum(jnp.where(owners[None, :] == slot[:, None], slot[None, :], 0), axis=1)
    came_from = jnp.arange(sites * sites, dtype=jnp.int32) // sites
    source = jnp.sum(jnp.where(site_bus[None, :] == wanted[:, None], came_from[None, :], 0), axis=1)
    owner = wanted // sites
    dz = (owner // (NC * NY) - source // (NC * NY)) % NZL
    dy = (owner // NC - source // NC) % NY
    core = site % NC
    beside = jnp.where(core == 0, 1, sites - 1)
    offset = jnp.remainder(owner - site, sites)
    table_of = jnp.where(offset == 0, 0, jnp.where(offset == beside, 1, 2))
    far_core = (source % NC != core).astype(jnp.int32)
    where = ((table_of * NC + far_core) * NZL + dz) * NY + dy

    def order_for(h):
        devices = h * NX + (x + jnp.arange(NX, dtype=jnp.int32)) % NX
        want = (devices[:, None] * per + jnp.arange(per, dtype=jnp.int32)[None, :]).reshape(-1)
        return jnp.sum(jnp.where(want[:, None] == slot[None, :], block_for[None, :], 0), axis=1)

    away = sketch_half(order_for(1 - half), ensemble, probes, block, 62)
    home = sketch_half(order_for(half), ensemble, probes, block, 62)
    sent = away[0]
    for d in range(1, NX):
        sent = sent + shift_x(away[d], d)
    crossed = swap_half(sent)
    around = [shift_x(home[d], d) for d in range(1, NX)]
    cuts, send, keep = gram_parts(place, home[0], *around, crossed)

    got = swap_core(send)
    pieces = add_and_split(place, 1, NY, [keep, got])
    cuts = exchange(shift_x, [after(c, pieces[0]) for c in cuts])
    part = total_of(exchange(shift_y, pieces))

    rows = len(cuts) * cuts[0].shape[0]
    blocks = turn(turn_y_kernel, place, [after(c, part) for c in cuts], [rows // NY] * NY, rows)
    parts = [part] + [shift_z(part, d) for d in range(1, NZL)]
    part = total_of([after(p, b) for p, b in zip(parts, blocks)])
    blocks = exchange(shift_y, blocks)

    part = part + swap_half(part)
    wide = jnp.concatenate([after(b, part) for b in blocks], axis=0)
    crossing = swap_half(wide)
    parts = [part] + [shift_x(part, d) for d in range(1, NX)]
    part = total_of([after(p, wide) for p in parts])

    parts = [part] + [shift_y(part, d) for d in range(1, NY)]
    blocks = turn(turn_z_kernel, place, [wide, after(crossing, part)], [2 * rows // NZL] * NZL, 2 * rows)
    run = join(place, 1, [after(p, b) for p, b in zip(parts, blocks)])
    blocks = exchange(shift_z, blocks)

    other = swap_core(run)
    inverse, unit = factor_open(place, run, other, n, 1)
    keep, pair = turn(
        functools.partial(turn_core_kernel, block), place, [after(b, inverse) for b in blocks], [rows] * 2
    )
    tables = [keep, swap_core(pair), pair, swap_core(keep), cross_chip(pair, True), cross_chip(keep, False)]
    inverse = factor_more(after(inverse, keep), 1, 3)
    parts = lines_part(where, [after(t, inverse) for t in tables], factors, lines // groups, block)
    parts = [parts[0]] + [shift_x(parts[d], -d) for d in range(1, NX)]
    inverse = factor_more(inverse, 3, 4)
    return finish(place, parts, inverse, unit, math.sqrt(site_rows * sites))


def solution(mesh):
    in_specs = (
        P("site", "samp"),
        P("samp", None),
        P(),
        P(("samp", "site"), None),
        P(("samp", "site"), None),
    )
    return jax.shard_map(
        per_device, mesh=mesh, in_specs=in_specs, out_specs=P(("samp", "site"), None), check_vma=False
    )
```

```python
import functools
import math

import jax
import jax.numpy as jnp
from jax import lax
from jax.experimental import pallas as pl
from jax.experimental.pallas import tpu as pltpu
from jax.sharding import PartitionSpec as P

FULL = lax.Precision.HIGHEST
F32 = jnp.float32
NX = 4
NZL = 4
NY = 4
NC = 2
UPPER = ((0, 0), (0, 1), (0, 2), (0, 3), (3, 3), (1, 1), (1, 2), (1, 3), (2, 2), (2, 3))
VMEM = pl.BlockSpec(memory_space=pltpu.VMEM)
SMEM = pl.BlockSpec(memory_space=pltpu.SMEM)


def params(mib=48):
    return pltpu.CompilerParams(vmem_limit_bytes=mib * 1024 * 1024)


def cost(flops, moved):
    return pl.CostEstimate(flops=flops, bytes_accessed=moved, transcendentals=0)


def shift_x(value, step):
    pairs = [(h * NX + x, h * NX + (x + step) % NX) for h in range(2) for x in range(NX)]
    return lax.ppermute(value, "samp", pairs)


def swap_half(value):
    return lax.ppermute(value, "samp", [(s, (s + NX) % (2 * NX)) for s in range(2 * NX)])


def site_index(z, y, c):
    return (z * NY + y) * NC + c


def shift_parts(value, dz, dy, dc):
    pairs = [
        (site_index(z, y, c), site_index((z + dz) % NZL, (y + dy) % NY, (c + dc) % NC))
        for z in range(NZL)
        for y in range(NY)
        for c in range(NC)
    ]
    return lax.ppermute(value, "site", pairs)


def sketch_kernel(count, order_ref, *refs):
    rows, probes_ref, outs = refs[:count], refs[count], refs[count + 1 :]
    step = pl.program_id(0)
    left = jnp.concatenate([r[...] for r in rows], axis=0)
    part = jnp.dot(left, probes_ref[...], preferred_element_type=F32)
    size = outs[0].shape[0]

    @pl.when(step == 0)
    def _():
        for d, out in enumerate(outs):
            out[...] = part[d * size : (d + 1) * size]

    @pl.when(step > 0)
    def _():
        for d, out in enumerate(outs):
            out[...] += part[d * size : (d + 1) * size]


def sketch_half(order, ensemble, probes, block, mib, depth=2048):
    count = order.shape[0]
    width = probes.shape[1]
    steps = ensemble.shape[1] // depth
    specs = [
        pl.BlockSpec((block, depth), functools.partial(lambda b, k, o: (o[b], k), b))
        for b in range(count)
    ]
    specs.append(pl.BlockSpec((depth, width), lambda k, o: (k, 0)))
    out_rows = count * block // NX
    return pl.pallas_call(
        functools.partial(sketch_kernel, count),
        grid_spec=pltpu.PrefetchScalarGridSpec(
            num_scalar_prefetch=1,
            grid=(steps,),
            in_specs=specs,
            out_specs=[pl.BlockSpec((out_rows, width), lambda k, o: (0, 0))] * NX,
        ),
        out_shape=[jax.ShapeDtypeStruct((out_rows, width), F32)] * NX,
        compiler_params=params(mib),
        cost_estimate=cost(2 * count * block * probes.size, 2 * (count * block * ensemble.shape[1] + probes.size)),
    )(order, *([ensemble] * count), probes)


def gram_kernel(place_ref, own_ref, a_ref, b_ref, c_ref, z_ref, *refs):
    cuts, (send_ref, keep_ref, whole, packed) = refs[:NX], refs[NX:]
    s = own_ref[...] + a_ref[...] + b_ref[...] + c_ref[...] + z_ref[...]
    whole[...] = s
    width = 128
    for d, cut in enumerate(cuts):
        cut[...] = whole[:, pl.ds(pl.multiple_of(lax.rem(place_ref[3] + d, NX) * width, width), width)]
    for r in range(4):
        row = lax.dot_general(
            s[:, r * width : (r + 1) * width], s[:, r * width :], (((0,), (0,)), ((), ())),
            precision=FULL, preferred_element_type=F32,
        )
        for slot, (p, q) in enumerate(UPPER):
            if p == r:
                packed[slot * width : (slot + 1) * width, :] = row[:, (q - r) * width : (q - r + 1) * width]
    half = packed.shape[0] // 2
    core = place_ref[0]
    send_ref[...] = packed[pl.ds(pl.multiple_of((1 - core) * half, half), half), :]
    keep_ref[...] = packed[pl.ds(pl.multiple_of(core * half, half), half), :]


def gram_parts(place, *parts):
    rows, width = parts[0].shape
    half = len(UPPER) * 128 // 2
    out = pl.pallas_call(
        gram_kernel,
        in_specs=[SMEM] + [VMEM] * 5,
        out_specs=[VMEM] * (NX + 2),
        out_shape=[jax.ShapeDtypeStruct((rows, width // NX), F32)] * NX
        + [jax.ShapeDtypeStruct((half, 128), F32)] * 2,
        scratch_shapes=[pltpu.VMEM((rows, width), F32), pltpu.VMEM((2 * half, 128), F32)],
        compiler_params=params(),
        cost_estimate=cost(6 * rows * width * width, 8 * rows * width * 4),
    )(place, *parts)
    return out[:NX], out[NX], out[NX + 1]


def split_kernel(axis, ways, place_ref, *refs):
    ins, outs, total = refs[:-ways - 1], refs[-ways - 1 : -1], refs[-1]
    acc = ins[0][...]
    for r in ins[1:]:
        acc = acc + r[...]
    total[...] = acc
    rows = outs[0].shape[0]
    me = place_ref[axis]
    for d, out in enumerate(outs):
        out[...] = total[pl.ds(pl.multiple_of(lax.rem(me + d, ways) * rows, 8), rows), :]


def add_and_split(place, axis, ways, parts):
    rows, width = parts[0].shape
    return pl.pallas_call(
        functools.partial(split_kernel, axis, ways),
        in_specs=[SMEM] + [VMEM] * len(parts),
        out_specs=[VMEM] * ways,
        out_shape=[jax.ShapeDtypeStruct((rows // ways, width), F32)] * ways,
        scratch_shapes=[pltpu.VMEM((rows, width), F32)],
        compiler_params=params(),
        cost_estimate=cost(rows * width * 4, rows * width * 16),
    )(place, *parts)


def join_kernel(axis, ways, place_ref, *refs):
    ins, out = refs[:-1], refs[-1]
    rows = ins[0].shape[0]
    me = place_ref[axis]
    for d, r in enumerate(ins):
        out[pl.ds(pl.multiple_of(lax.rem(me - d + ways, ways) * rows, 8), rows), :] = r[...]


def join(place, axis, parts):
    rows, width = parts[0].shape
    ways = len(parts)
    return pl.pallas_call(
        functools.partial(join_kernel, axis, ways),
        in_specs=[SMEM] + [VMEM] * ways,
        out_specs=VMEM,
        out_shape=jax.ShapeDtypeStruct((rows * ways, width), F32),
        compiler_params=params(),
        cost_estimate=cost(0, rows * ways * width * 8),
    )(place, *parts)


def after(value, other):
    return lax.optimization_barrier((value, other))[0]


def exchange(move, pieces):
    return [pieces[0]] + [move(pieces[d], d) for d in range(1, len(pieces))]


def total_of(parts):
    out = parts[0]
    for p in parts[1:]:
        out = out + p
    return out


def shift_y(value, d):
    return shift_parts(value, 0, d, 0)


def shift_z(value, d):
    return shift_parts(value, d, 0, 0)


def swap_core(value):
    return shift_parts(value, 0, 0, 1)


def turn_y_kernel(place_ref, *refs):
    ins, outs, whole = refs[:NX], refs[NX:-1], refs[-1]
    rows = ins[0].shape[0]
    for d, r in enumerate(ins):
        whole[pl.ds(pl.multiple_of(lax.rem(place_ref[3] - d + NX, NX) * rows, 8), rows), :] = r[...]
    size = outs[0].shape[0] // 2
    for d, out in enumerate(outs):
        at = lax.rem(place_ref[1] + d, NY) * size
        for z in range(2):
            out[z * size : (z + 1) * size, :] = whole[pl.ds(pl.multiple_of(z * 2 * rows + at, 8), size), :]


def turn_z_kernel(place_ref, mine_ref, theirs_ref, *refs):
    outs, whole = refs[:-1], refs[-1]
    rows = mine_ref.shape[0]
    half = place_ref[4]
    whole[pl.ds(pl.multiple_of(half * rows, 8), rows), :] = mine_ref[...]
    whole[pl.ds(pl.multiple_of((1 - half) * rows, 8), rows), :] = theirs_ref[...]
    size = rows // (2 * NY)
    for d, out in enumerate(outs):
        to = lax.rem(place_ref[2] + d, NZL)
        at = to // 2 * rows + to % 2 * size
        for y in range(NY):
            out[y * size : (y + 1) * size, :] = whole[pl.ds(pl.multiple_of(at + y * 2 * size, 8), size), :]


def turn_core_kernel(block, place_ref, *refs):
    ins, (keep, pair, both) = refs[:NZL], refs[NZL:]
    rows = keep.shape[0]
    core = place_ref[0]
    count = ins[0].shape[0] // (NC * block)
    for z, r in enumerate(ins):
        for y in range(count):
            row = (z * count + y) * block
            mine = r[pl.ds(pl.multiple_of((y * NC + core) * block, 8), block), :]
            theirs = r[pl.ds(pl.multiple_of((y * NC + 1 - core) * block, 8), block), :]
            keep[row : row + block, :] = mine
            pair[row : row + block, :] = theirs
            both[row : row + block, :] = theirs
            both[rows + row : rows + row + block, :] = mine


def turn(kernel, place, parts, shapes, scratch_rows=0):
    width = parts[0].shape[1]
    moved = 8 * sum(p.size for p in parts)
    return pl.pallas_call(
        kernel,
        in_specs=[SMEM] + [VMEM] * len(parts),
        out_specs=[VMEM] * len(shapes),
        out_shape=[jax.ShapeDtypeStruct((r, width), F32) for r in shapes],
        scratch_shapes=[pltpu.VMEM((scratch_rows, width), F32)] if scratch_rows else [],
        compiler_params=params(),
        cost_estimate=cost(0, moved),
    )(place, *parts)


def cross_chip(value, same_core):
    chips = NZL * NY
    pairs = []
    for p in range(chips):
        up, down = (p + 1) % chips * NC, (p - 1) % chips * NC + 1
        pairs += [(p * NC, up), (p * NC + 1, down)] if same_core else [(p * NC + 1, up), (p * NC, down)]
    return lax.ppermute(value, "site", pairs)


def block_inverse(tile_rows, size, lane):
    rows = list(tile_rows)
    done = [[] for _ in rows]
    sub = lax.broadcasted_iota(jnp.int32, (8, size), 0)

    def wide(v, at):
        return jnp.broadcast_to(v[:, at : at + 1], (8, size))

    def tall(j):
        q, o = divmod(j, 8)
        return [jnp.broadcast_to(rows[q][o + a : o + a + 1, :], (8, size)) for a in range(4)]

    spread = tall(0)
    s = [[wide(spread[a], b) if b >= a else None for b in range(4)] for a in range(4)]
    for j in range(0, size, 4):
        q, o = divmod(j, 8)
        in_block = (lane >= j) & (lane < j + 4)
        up = [jnp.where(in_block, jnp.where(lane == j + a, 1.0, 0.0), spread[a]) for a in range(4)]
        a, b, c = s[0][0], s[0][1], s[1][1]
        e, f, g, h = s[0][2], s[1][2], s[0][3], s[1][3]
        inv1 = 1.0 / (a * c - b * b)
        n20, n21 = e * c - f * b, f * a - e * b
        n30, n31 = g * c - h * b, h * a - g * b
        s22 = s[2][2] - inv1 * (n20 * e + n21 * f)
        s23 = s[2][3] - inv1 * (n20 * g + n21 * h)
        s33 = s[3][3] - inv1 * (n30 * g + n31 * h)
        w20, w21, w30, w31 = n20 * inv1, n21 * inv1, n30 * inv1, n31 * inv1
        ca, cb, cc = c * inv1, b * inv1, a * inv1
        inv2 = 1.0 / (s22 * s33 - s23 * s23)

        def solve(t0, t1, t2, t3):
            u2 = t2 - (w20 * t0 + w21 * t1)
            u3 = t3 - (w30 * t0 + w31 * t1)
            v2 = inv2 * (s33 * u2 - s23 * u3)
            v3 = inv2 * (s22 * u3 - s23 * u2)
            v0 = (ca * t0 - cb * t1) - (w20 * v2 + w30 * v3)
            v1 = (cc * t1 - cb * t0) - (w21 * v2 + w31 * v3)
            return v0, v1, v2, v3

        v = solve(*up)
        more = j + 4 < size
        if more:
            cross = [[wide(spread[k], j + 4 + m) for m in range(4)] for k in range(4)]
            coming = tall(j + 4)
            nexts = [[None] * 4 for _ in range(4)]
            for m in range(4):
                vm = solve(cross[0][m], cross[1][m], cross[2][m], cross[3][m])
                for l in range(m + 1):
                    nexts[l][m] = wide(coming[l], j + 4 + m) - (
                        (cross[0][l] * vm[0] + cross[1][l] * vm[1]) + (cross[2][l] * vm[2] + cross[3][l] * vm[3])
                    )
            ahead = [
                jnp.where(in_block, 0.0, coming[m])
                - ((cross[0][m] * v[0] + cross[1][m] * v[1]) + (cross[2][m] * v[2] + cross[3][m] * v[3]))
                for m in range(4)
            ]
        for t in range(q + (1 if o == 4 else 0), len(rows)):
            cur = rows[t]
            new = jnp.where(in_block, 0.0, cur) - (
                (wide(cur, j) * v[0] + wide(cur, j + 1) * v[1]) + (wide(cur, j + 2) * v[2] + wide(cur, j + 3) * v[3])
            )
            rows[t] = jnp.where(sub >= o + 4, new, cur) if t == q else new
        r0 = lax.rsqrt(a)
        m1 = b * (r0 * r0)
        r1 = lax.rsqrt(c - m1 * b)
        r2 = lax.rsqrt(s22)
        m3 = s23 * (r2 * r2)
        r3 = lax.rsqrt(s33 - m3 * s23)
        u2 = up[2] - (w20 * up[0] + w21 * up[1])
        u3 = up[3] - (w30 * up[0] + w31 * up[1])
        done[q] += [r0 * up[0], r1 * (up[1] - m1 * up[0]), r2 * u2, r3 * (u3 - m3 * u2)]
        if more:
            spread, s = ahead, nexts
    out = []
    for q, parts in enumerate(done):
        whole = parts[0]
        for k in range(1, 8):
            whole = jnp.where(sub == k, parts[k], whole)
        out.append(jnp.where(lane <= sub + 8 * q, whole, 0.0))
    return out


def factor_steps(x_ref, first, last):
    width = 128
    n = x_ref.shape[0]
    steps = n // width
    lane = lax.broadcasted_iota(jnp.int32, (8, width), 1)
    for k in range(first, last):
        lo, hi = k * width, (k + 1) * width
        tiles = [x_ref[lo + 8 * t : lo + 8 * t + 8, lo:hi] for t in range(width // 8)]
        inv = jnp.concatenate(block_inverse(tiles, width, lane), axis=0)
        if k > 0:
            x_ref[lo:hi, :lo] = jnp.dot(inv, x_ref[lo:hi, :lo], precision=FULL, preferred_element_type=F32)
        x_ref[lo:hi, lo:hi] = inv
        if k < steps - 1:
            upper = jnp.dot(inv, x_ref[lo:hi, hi:], precision=FULL, preferred_element_type=F32)
            x_ref[lo:hi, hi:] = upper
            x_ref[hi:, lo:hi] = jnp.zeros((n - hi, width), F32)
            x_ref[hi:, :] -= lax.dot_general(
                upper, x_ref[lo:hi, :], (((0,), (0,)), ((), ())), precision=FULL, preferred_element_type=F32
            )
            x_ref[lo:hi, hi:] = jnp.zeros((width, n - hi), F32)


def factor_open_kernel(last, place_ref, half_ref, other_ref, x_ref, scale_ref, packed):
    width = 128
    n = x_ref.shape[0]
    half = half_ref.shape[0]
    core = place_ref[0]
    packed[pl.ds(pl.multiple_of(core * half, half), half), :] = half_ref[...]
    packed[pl.ds(pl.multiple_of((1 - core) * half, half), half), :] = other_ref[...]
    x_ref[...] = jnp.zeros((n, n), F32)
    eye = lax.broadcasted_iota(jnp.int32, (width, width), 0) == lax.broadcasted_iota(jnp.int32, (width, width), 1)
    across, down = [], []
    for k in range(n // width):
        slot = UPPER.index((k, k))
        diag = jnp.where(eye, packed[slot * width : (slot + 1) * width, :], 0.0)
        across.append(lax.rsqrt(jnp.sum(diag, axis=0, keepdims=True)))
        down.append(lax.rsqrt(jnp.sum(diag, axis=1, keepdims=True)))
        scale_ref[:, k * width : (k + 1) * width] = jnp.broadcast_to(across[k], (8, width))
    for slot, (p, q) in enumerate(UPPER):
        x_ref[p * width : (p + 1) * width, q * width : (q + 1) * width] = (
            packed[slot * width : (slot + 1) * width, :] * down[p] * across[q]
        )
    factor_steps(x_ref, 0, last)


def factor_open(place, half, other, n, last):
    return pl.pallas_call(
        functools.partial(factor_open_kernel, last),
        in_specs=[SMEM, VMEM, VMEM],
        out_specs=[VMEM] * 2,
        out_shape=[jax.ShapeDtypeStruct((n, n), F32), jax.ShapeDtypeStruct((8, n), F32)],
        scratch_shapes=[pltpu.VMEM((2 * half.shape[0], 128), F32)],
        compiler_params=params(),
        cost_estimate=cost(10 * last * n * n * n, 8 * n * n),
    )(place, half, other)


def factor_more_kernel(first, last, in_ref, x_ref):
    x_ref[...] = in_ref[...]
    factor_steps(x_ref, first, last)


def factor_more(value, first, last):
    n = value.shape[0]
    return pl.pallas_call(
        functools.partial(factor_more_kernel, first, last),
        in_specs=[VMEM],
        out_specs=VMEM,
        out_shape=jax.ShapeDtypeStruct((n, n), F32),
        compiler_params=params(),
        cost_estimate=cost(10 * (last - first) * n * n * n, 8 * n * n),
    )(value)


def lines_kernel(count, group, block, where_ref, *refs):
    tables, refs = refs[:count], refs[count:]
    factors, outs, top, rest = refs[:NX], refs[NX : 2 * NX], refs[-2], refs[-1]
    at = 0
    for table in tables:
        value = table[...]
        first = value.astype(jnp.bfloat16)
        top[at : at + table.shape[0], :] = first
        rest[at : at + table.shape[0], :] = (value - first.astype(F32)).astype(jnp.bfloat16)
        at += table.shape[0]
    lines, span = factors[0].shape
    links = span // block
    groups = lines // group
    for d in range(NX):

        def one(g, carry, d=d):
            at = [
                pl.multiple_of(where_ref[(d * groups + g) * links + t] * block, block) for t in range(links)
            ]
            line = pl.ds(pl.multiple_of(g * group, group), group)
            f = factors[d][line, :].astype(jnp.bfloat16)
            first = jnp.concatenate([top[pl.ds(a, block), :] for a in at], axis=0)
            second = jnp.concatenate([rest[pl.ds(a, block), :] for a in at], axis=0)
            outs[d][line, :] = jnp.dot(f, first, preferred_element_type=F32) + jnp.dot(
                f, second, preferred_element_type=F32
            )
            return carry

        lax.fori_loop(0, groups, one, 0, unroll=True)


def lines_part(where, tables, factors, group, block):
    rows, width = sum(t.shape[0] for t in tables), tables[0].shape[1]
    lines = factors[0].shape[0]
    return pl.pallas_call(
        functools.partial(lines_kernel, len(tables), group, block),
        in_specs=[SMEM] + [VMEM] * (len(tables) + NX),
        out_specs=[VMEM] * NX,
        out_shape=[jax.ShapeDtypeStruct((lines, width), F32)] * NX,
        scratch_shapes=[pltpu.VMEM((rows, width), jnp.bfloat16)] * 2,
        compiler_params=params(),
        cost_estimate=cost(64 * lines * width * NX * 256, 4 * rows * width),
    )(where, *tables, *factors)


def finish_kernel(scale, place_ref, *refs):
    ins, (x_ref, unit_ref, out_ref, wide) = refs[:NX], refs[NX:]
    width = ins[0].shape[1]
    me = place_ref[3]
    for d, r in enumerate(ins):
        wide[:, pl.ds(pl.multiple_of(lax.rem(me + d, NX) * width, width), width)] = r[...]
    pairs = []
    for value in (wide[...] * (scale * unit_ref[0:1, :]), x_ref[...]):
        top = value.astype(jnp.bfloat16)
        pairs.append((top, (value - top.astype(F32)).astype(jnp.bfloat16)))
    (a, a_rest), (b, b_rest) = pairs

    def product(p, q):
        return lax.dot_general(p, q, (((1,), (1,)), ((), ())), preferred_element_type=F32)

    out_ref[...] = product(a, b) + (product(a, b_rest) + product(a_rest, b))


def finish(place, parts, inverse, unit, scale):
    lines = parts[0].shape[0]
    n = inverse.shape[0]
    return pl.pallas_call(
        functools.partial(finish_kernel, scale),
        in_specs=[SMEM] + [VMEM] * (NX + 2),
        out_specs=VMEM,
        out_shape=jax.ShapeDtypeStruct((lines, n), F32),
        scratch_shapes=[pltpu.VMEM((lines, n), F32)],
        compiler_params=params(),
        cost_estimate=cost(12 * lines * n * n, 8 * n * n),
    )(place, *parts, inverse, unit)


def per_device(ensemble, probes, site_bus, incidence, shift_factors):
    sites = lax.axis_size("site")
    samps = lax.axis_size("samp")
    site = lax.axis_index("site")
    samp = lax.axis_index("samp")
    site_rows = ensemble.shape[0]
    n = probes.shape[1]
    block = site_rows // sites
    per = sites // samps
    half, x = samp // NX, samp % NX
    place = jnp.stack([site % NC, site // NC % NY, site // (NC * NY), x, half]).astype(jnp.int32)

    lines, span = shift_factors.shape
    groups, links = incidence.shape
    lists = jnp.pad(incidence.astype(F32), ((0, 0), (0, span - links)))
    carried = jnp.concatenate([shift_factors.astype(F32), lists], axis=0)

    owners = lax.dynamic_slice_in_dim(site_bus, site * sites, sites) // sites
    slot = jnp.arange(sites, dtype=jnp.int32)
    block_for = jnp.sum(jnp.where(owners[None, :] == slot[:, None], slot[None, :], 0), axis=1)

    def order_for(h):
        devices = h * NX + (x + jnp.arange(NX, dtype=jnp.int32)) % NX
        want = (devices[:, None] * per + jnp.arange(per, dtype=jnp.int32)[None, :]).reshape(-1)
        return jnp.sum(jnp.where(want[:, None] == slot[None, :], block_for[None, :], 0), axis=1)

    away = sketch_half(order_for(1 - half), ensemble, probes, block, 48)
    home = sketch_half(order_for(half), ensemble, probes, block, 48)
    sent = total_of([after(p, home[0]) for p in exchange(shift_x, away)])
    crossed = swap_half(sent)
    around = [shift_x(home[d], d) for d in range(1, NX)]
    carried = exchange(shift_x, [after(carried, sent)] * NX)
    cuts, send, keep = gram_parts(place, home[0], *around, after(crossed, carried[1:]))
    factors = [c[:lines] for c in carried]
    wanted = jnp.stack([c[lines:, :links] for c in carried]).astype(jnp.int32).reshape(-1)
    came_from = jnp.arange(sites * sites, dtype=jnp.int32) // sites
    source = jnp.sum(jnp.where(site_bus[None, :] == wanted[:, None], came_from[None, :], 0), axis=1)
    owner = wanted // sites
    dz = (owner // (NC * NY) - source // (NC * NY)) % NZL
    dy = (owner // NC - source // NC) % NY
    core = site % NC
    beside = jnp.where(core == 0, 1, sites - 1)
    offset = jnp.remainder(owner - site, sites)
    table_of = jnp.where(offset == 0, 0, jnp.where(offset == beside, 1, 2))
    far_core = (source % NC != core).astype(jnp.int32)
    place_of = jnp.where(table_of == 2, 4 + far_core, far_core * 2 + table_of)
    where = (place_of * NZL + dz) * NY + dy

    got = swap_core(send)
    pieces = add_and_split(place, 1, NY, [keep, got])
    cuts = exchange(shift_x, [after(c, pieces[0]) for c in cuts])
    part = total_of(exchange(shift_y, pieces))

    rows = len(cuts) * cuts[0].shape[0]
    blocks = turn(turn_y_kernel, place, [after(c, part) for c in cuts], [rows // NY] * NY, rows)
    parts = [part] + [shift_z(part, d) for d in range(1, NZL)]
    part = total_of([after(p, b) for p, b in zip(parts, blocks)])
    blocks = exchange(shift_y, blocks)

    part = part + swap_half(part)
    wide = jnp.concatenate([after(b, part) for b in blocks], axis=0)
    crossing = swap_half(wide)
    parts = [part] + [shift_x(part, d) for d in range(1, NX)]
    part = total_of([after(p, wide) for p in parts])

    parts = [part] + [shift_y(part, d) for d in range(1, NY)]
    blocks = turn(turn_z_kernel, place, [wide, after(crossing, part)], [2 * rows // NZL] * NZL, 2 * rows)
    run = join(place, 1, [after(p, b) for p, b in zip(parts, blocks)])
    blocks = exchange(shift_z, blocks)

    other = swap_core(run)
    inverse, unit = factor_open(place, run, other, n, 1)
    keep, pair, both = turn(
        functools.partial(turn_core_kernel, block), place, [after(b, inverse) for b in blocks], [rows, rows, 2 * rows]
    )
    tables = [keep, pair, swap_core(both), cross_chip(pair, True), cross_chip(keep, False)]
    inverse = factor_more(after(inverse, keep), 1, 3)
    parts = lines_part(where, [after(t, inverse) for t in tables], factors, lines // groups, block)
    parts = [parts[0]] + [shift_x(parts[d], -d) for d in range(1, NX)]
    inverse = factor_more(inverse, 3, 4)
    return finish(place, parts, inverse, unit, math.sqrt(site_rows * sites))


def solution(mesh):
    in_specs = (
        P("site", "samp"),
        P("samp", None),
        P(),
        P(("samp", "site"), None),
        P(("samp", "site"), None),
    )
    return jax.shard_map(
        per_device, mesh=mesh, in_specs=in_specs, out_specs=P(("samp", "site"), None), check_vma=False
    )
```

```python
import functools
import math

import jax
import jax.numpy as jnp
from jax import lax
from jax.experimental import pallas as pl
from jax.experimental.pallas import tpu as pltpu
from jax.sharding import PartitionSpec as P

FULL = lax.Precision.HIGHEST
F32 = jnp.float32
NX = 4
NZL = 4
NY = 4
NC = 2
UPPER = ((0, 0), (0, 1), (0, 2), (0, 3), (3, 3), (1, 1), (1, 2), (1, 3), (2, 2), (2, 3))
VMEM = pl.BlockSpec(memory_space=pltpu.VMEM)
SMEM = pl.BlockSpec(memory_space=pltpu.SMEM)


def params(mib=48):
    return pltpu.CompilerParams(vmem_limit_bytes=mib * 1024 * 1024)


def cost(flops, moved):
    return pl.CostEstimate(flops=flops, bytes_accessed=moved, transcendentals=0)


def shift_x(value, step):
    pairs = [(h * NX + x, h * NX + (x + step) % NX) for h in range(2) for x in range(NX)]
    return lax.ppermute(value, "samp", pairs)


def swap_half(value):
    return lax.ppermute(value, "samp", [(s, (s + NX) % (2 * NX)) for s in range(2 * NX)])


def site_index(z, y, c):
    return (z * NY + y) * NC + c


def shift_parts(value, dz, dy, dc):
    pairs = [
        (site_index(z, y, c), site_index((z + dz) % NZL, (y + dy) % NY, (c + dc) % NC))
        for z in range(NZL)
        for y in range(NY)
        for c in range(NC)
    ]
    return lax.ppermute(value, "site", pairs)


def sketch_kernel(count, order_ref, *refs):
    rows, probes_ref, outs = refs[:count], refs[count], refs[count + 1 :]
    step = pl.program_id(0)
    left = jnp.concatenate([r[...] for r in rows], axis=0)
    part = jnp.dot(left, probes_ref[...], preferred_element_type=F32)
    size = outs[0].shape[0]

    @pl.when(step == 0)
    def _():
        for d, out in enumerate(outs):
            out[...] = part[d * size : (d + 1) * size]

    @pl.when(step > 0)
    def _():
        for d, out in enumerate(outs):
            out[...] += part[d * size : (d + 1) * size]


def sketch_half(order, ensemble, probes, block, mib, depth=2048):
    count = order.shape[0]
    width = probes.shape[1]
    steps = ensemble.shape[1] // depth
    specs = [
        pl.BlockSpec((block, depth), functools.partial(lambda b, k, o: (o[b], k), b))
        for b in range(count)
    ]
    specs.append(pl.BlockSpec((depth, width), lambda k, o: (k, 0)))
    out_rows = count * block // NX
    return pl.pallas_call(
        functools.partial(sketch_kernel, count),
        grid_spec=pltpu.PrefetchScalarGridSpec(
            num_scalar_prefetch=1,
            grid=(steps,),
            in_specs=specs,
            out_specs=[pl.BlockSpec((out_rows, width), lambda k, o: (0, 0))] * NX,
        ),
        out_shape=[jax.ShapeDtypeStruct((out_rows, width), F32)] * NX,
        compiler_params=params(mib),
        cost_estimate=cost(2 * count * block * probes.size, 2 * (count * block * ensemble.shape[1] + probes.size)),
    )(order, *([ensemble] * count), probes)


def gram_kernel(place_ref, own_ref, a_ref, b_ref, c_ref, z_ref, *refs):
    cuts, (send_ref, keep_ref, whole, packed) = refs[:NX], refs[NX:]
    s = own_ref[...] + a_ref[...] + b_ref[...] + c_ref[...] + z_ref[...]
    whole[...] = s
    width = 128
    for d, cut in enumerate(cuts):
        cut[...] = whole[:, pl.ds(pl.multiple_of(lax.rem(place_ref[3] + d, NX) * width, width), width)]
    for r in range(4):
        row = lax.dot_general(
            s[:, r * width : (r + 1) * width], s[:, r * width :], (((0,), (0,)), ((), ())),
            precision=FULL, preferred_element_type=F32,
        )
        for slot, (p, q) in enumerate(UPPER):
            if p == r:
                packed[slot * width : (slot + 1) * width, :] = row[:, (q - r) * width : (q - r + 1) * width]
    half = packed.shape[0] // 2
    core = place_ref[0]
    send_ref[...] = packed[pl.ds(pl.multiple_of((1 - core) * half, half), half), :]
    keep_ref[...] = packed[pl.ds(pl.multiple_of(core * half, half), half), :]


def gram_parts(place, *parts):
    rows, width = parts[0].shape
    half = len(UPPER) * 128 // 2
    out = pl.pallas_call(
        gram_kernel,
        in_specs=[SMEM] + [VMEM] * 5,
        out_specs=[VMEM] * (NX + 2),
        out_shape=[jax.ShapeDtypeStruct((rows, width // NX), F32)] * NX
        + [jax.ShapeDtypeStruct((half, 128), F32)] * 2,
        scratch_shapes=[pltpu.VMEM((rows, width), F32), pltpu.VMEM((2 * half, 128), F32)],
        compiler_params=params(),
        cost_estimate=cost(6 * rows * width * width, 8 * rows * width * 4),
    )(place, *parts)
    return out[:NX], out[NX], out[NX + 1]


def split_kernel(axis, ways, place_ref, *refs):
    ins, outs, total = refs[:-ways - 1], refs[-ways - 1 : -1], refs[-1]
    acc = ins[0][...]
    for r in ins[1:]:
        acc = acc + r[...]
    total[...] = acc
    rows = outs[0].shape[0]
    me = place_ref[axis]
    for d, out in enumerate(outs):
        out[...] = total[pl.ds(pl.multiple_of(lax.rem(me + d, ways) * rows, 8), rows), :]


def add_and_split(place, axis, ways, parts):
    rows, width = parts[0].shape
    return pl.pallas_call(
        functools.partial(split_kernel, axis, ways),
        in_specs=[SMEM] + [VMEM] * len(parts),
        out_specs=[VMEM] * ways,
        out_shape=[jax.ShapeDtypeStruct((rows // ways, width), F32)] * ways,
        scratch_shapes=[pltpu.VMEM((rows, width), F32)],
        compiler_params=params(),
        cost_estimate=cost(rows * width * 4, rows * width * 16),
    )(place, *parts)


def join_kernel(axis, ways, place_ref, *refs):
    ins, out = refs[:-1], refs[-1]
    rows = ins[0].shape[0]
    me = place_ref[axis]
    for d, r in enumerate(ins):
        out[pl.ds(pl.multiple_of(lax.rem(me - d + ways, ways) * rows, 8), rows), :] = r[...]


def join(place, axis, parts):
    rows, width = parts[0].shape
    ways = len(parts)
    return pl.pallas_call(
        functools.partial(join_kernel, axis, ways),
        in_specs=[SMEM] + [VMEM] * ways,
        out_specs=VMEM,
        out_shape=jax.ShapeDtypeStruct((rows * ways, width), F32),
        compiler_params=params(),
        cost_estimate=cost(0, rows * ways * width * 8),
    )(place, *parts)


def after(value, other):
    return lax.optimization_barrier((value, other))[0]


def exchange(move, pieces):
    return [pieces[0]] + [move(pieces[d], d) for d in range(1, len(pieces))]


def total_of(parts):
    out = parts[0]
    for p in parts[1:]:
        out = out + p
    return out


def shift_y(value, d):
    return shift_parts(value, 0, d, 0)


def shift_z(value, d):
    return shift_parts(value, d, 0, 0)


def swap_core(value):
    return shift_parts(value, 0, 0, 1)


def turn_y_kernel(place_ref, *refs):
    ins, outs, whole = refs[:NX], refs[NX:-1], refs[-1]
    rows = ins[0].shape[0]
    for d, r in enumerate(ins):
        whole[pl.ds(pl.multiple_of(lax.rem(place_ref[3] - d + NX, NX) * rows, 8), rows), :] = r[...]
    size = outs[0].shape[0] // 2
    for d, out in enumerate(outs):
        at = lax.rem(place_ref[1] + d, NY) * size
        for z in range(2):
            out[z * size : (z + 1) * size, :] = whole[pl.ds(pl.multiple_of(z * 2 * rows + at, 8), size), :]


def turn_z_kernel(place_ref, mine_ref, theirs_ref, *refs):
    outs, whole = refs[:-1], refs[-1]
    rows = mine_ref.shape[0]
    half = place_ref[4]
    whole[pl.ds(pl.multiple_of(half * rows, 8), rows), :] = mine_ref[...]
    whole[pl.ds(pl.multiple_of((1 - half) * rows, 8), rows), :] = theirs_ref[...]
    size = rows // (2 * NY)
    for d, out in enumerate(outs):
        to = lax.rem(place_ref[2] + d, NZL)
        at = to // 2 * rows + to % 2 * size
        for y in range(NY):
            out[y * size : (y + 1) * size, :] = whole[pl.ds(pl.multiple_of(at + y * 2 * size, 8), size), :]


def turn_core_kernel(block, place_ref, *refs):
    ins, (keep, pair, both) = refs[:NZL], refs[NZL:]
    rows = keep.shape[0]
    core = place_ref[0]
    count = ins[0].shape[0] // (NC * block)
    for z, r in enumerate(ins):
        for y in range(count):
            row = (z * count + y) * block
            mine = r[pl.ds(pl.multiple_of((y * NC + core) * block, 8), block), :]
            theirs = r[pl.ds(pl.multiple_of((y * NC + 1 - core) * block, 8), block), :]
            keep[row : row + block, :] = mine
            pair[row : row + block, :] = theirs
            both[row : row + block, :] = theirs
            both[rows + row : rows + row + block, :] = mine


def turn(kernel, place, parts, shapes, scratch_rows=0):
    width = parts[0].shape[1]
    moved = 8 * sum(p.size for p in parts)
    return pl.pallas_call(
        kernel,
        in_specs=[SMEM] + [VMEM] * len(parts),
        out_specs=[VMEM] * len(shapes),
        out_shape=[jax.ShapeDtypeStruct((r, width), F32) for r in shapes],
        scratch_shapes=[pltpu.VMEM((scratch_rows, width), F32)] if scratch_rows else [],
        compiler_params=params(),
        cost_estimate=cost(0, moved),
    )(place, *parts)


def cross_chip(value, same_core):
    chips = NZL * NY
    pairs = []
    for p in range(chips):
        up, down = (p + 1) % chips * NC, (p - 1) % chips * NC + 1
        pairs += [(p * NC, up), (p * NC + 1, down)] if same_core else [(p * NC + 1, up), (p * NC, down)]
    return lax.ppermute(value, "site", pairs)


def block_inverse(tile_rows, size, lane):
    rows = list(tile_rows)
    done = [[] for _ in rows]
    sub = lax.broadcasted_iota(jnp.int32, (8, size), 0)

    def wide(v, at):
        return jnp.broadcast_to(v[:, at : at + 1], (8, size))

    def tall(j):
        q, o = divmod(j, 8)
        return [jnp.broadcast_to(rows[q][o + a : o + a + 1, :], (8, size)) for a in range(4)]

    spread = tall(0)
    s = [[wide(spread[a], b) if b >= a else None for b in range(4)] for a in range(4)]
    for j in range(0, size, 4):
        q, o = divmod(j, 8)
        in_block = (lane >= j) & (lane < j + 4)
        up = [jnp.where(in_block, jnp.where(lane == j + a, 1.0, 0.0), spread[a]) for a in range(4)]
        a, b, c = s[0][0], s[0][1], s[1][1]
        e, f, g, h = s[0][2], s[1][2], s[0][3], s[1][3]
        inv1 = 1.0 / (a * c - b * b)
        n20, n21 = e * c - f * b, f * a - e * b
        n30, n31 = g * c - h * b, h * a - g * b
        s22 = s[2][2] - inv1 * (n20 * e + n21 * f)
        s23 = s[2][3] - inv1 * (n20 * g + n21 * h)
        s33 = s[3][3] - inv1 * (n30 * g + n31 * h)
        w20, w21, w30, w31 = n20 * inv1, n21 * inv1, n30 * inv1, n31 * inv1
        ca, cb, cc = c * inv1, b * inv1, a * inv1
        inv2 = 1.0 / (s22 * s33 - s23 * s23)

        def solve(t0, t1, t2, t3):
            u2 = t2 - (w20 * t0 + w21 * t1)
            u3 = t3 - (w30 * t0 + w31 * t1)
            v2 = inv2 * (s33 * u2 - s23 * u3)
            v3 = inv2 * (s22 * u3 - s23 * u2)
            v0 = (ca * t0 - cb * t1) - (w20 * v2 + w30 * v3)
            v1 = (cc * t1 - cb * t0) - (w21 * v2 + w31 * v3)
            return v0, v1, v2, v3

        v = solve(*up)
        more = j + 4 < size
        if more:
            cross = [[wide(spread[k], j + 4 + m) for m in range(4)] for k in range(4)]
            coming = tall(j + 4)
            nexts = [[None] * 4 for _ in range(4)]
            for m in range(4):
                vm = solve(cross[0][m], cross[1][m], cross[2][m], cross[3][m])
                for l in range(m + 1):
                    nexts[l][m] = wide(coming[l], j + 4 + m) - (
                        (cross[0][l] * vm[0] + cross[1][l] * vm[1]) + (cross[2][l] * vm[2] + cross[3][l] * vm[3])
                    )
            ahead = [
                jnp.where(in_block, 0.0, coming[m])
                - ((cross[0][m] * v[0] + cross[1][m] * v[1]) + (cross[2][m] * v[2] + cross[3][m] * v[3]))
                for m in range(4)
            ]
        for t in range(q + (1 if o == 4 else 0), len(rows)):
            cur = rows[t]
            new = jnp.where(in_block, 0.0, cur) - (
                (wide(cur, j) * v[0] + wide(cur, j + 1) * v[1]) + (wide(cur, j + 2) * v[2] + wide(cur, j + 3) * v[3])
            )
            rows[t] = jnp.where(sub >= o + 4, new, cur) if t == q else new
        r0 = lax.rsqrt(a)
        m1 = b * (r0 * r0)
        r1 = lax.rsqrt(c - m1 * b)
        r2 = lax.rsqrt(s22)
        m3 = s23 * (r2 * r2)
        r3 = lax.rsqrt(s33 - m3 * s23)
        u2 = up[2] - (w20 * up[0] + w21 * up[1])
        u3 = up[3] - (w30 * up[0] + w31 * up[1])
        done[q] += [r0 * up[0], r1 * (up[1] - m1 * up[0]), r2 * u2, r3 * (u3 - m3 * u2)]
        if more:
            spread, s = ahead, nexts
    out = []
    for q, parts in enumerate(done):
        whole = parts[0]
        for k in range(1, 8):
            whole = jnp.where(sub == k, parts[k], whole)
        out.append(jnp.where(lane <= sub + 8 * q, whole, 0.0))
    return out


def factor_steps(x_ref, first, last):
    width = 128
    n = x_ref.shape[0]
    steps = n // width
    lane = lax.broadcasted_iota(jnp.int32, (8, width), 1)
    for k in range(first, last):
        lo, hi = k * width, (k + 1) * width
        tiles = [x_ref[lo + 8 * t : lo + 8 * t + 8, lo:hi] for t in range(width // 8)]
        inv = jnp.concatenate(block_inverse(tiles, width, lane), axis=0)
        if k > 0:
            x_ref[lo:hi, :lo] = jnp.dot(inv, x_ref[lo:hi, :lo], precision=FULL, preferred_element_type=F32)
        x_ref[lo:hi, lo:hi] = inv
        if k < steps - 1:
            upper = jnp.dot(inv, x_ref[lo:hi, hi:], precision=FULL, preferred_element_type=F32)
            x_ref[lo:hi, hi:] = upper
            x_ref[hi:, lo:hi] = jnp.zeros((n - hi, width), F32)
            x_ref[hi:, :] -= lax.dot_general(
                upper, x_ref[lo:hi, :], (((0,), (0,)), ((), ())), precision=FULL, preferred_element_type=F32
            )
            x_ref[lo:hi, hi:] = jnp.zeros((width, n - hi), F32)


def factor_open_kernel(last, place_ref, half_ref, other_ref, x_ref, scale_ref, packed):
    width = 128
    n = x_ref.shape[0]
    half = half_ref.shape[0]
    core = place_ref[0]
    packed[pl.ds(pl.multiple_of(core * half, half), half), :] = half_ref[...]
    packed[pl.ds(pl.multiple_of((1 - core) * half, half), half), :] = other_ref[...]
    x_ref[...] = jnp.zeros((n, n), F32)
    eye = lax.broadcasted_iota(jnp.int32, (width, width), 0) == lax.broadcasted_iota(jnp.int32, (width, width), 1)
    across, down = [], []
    for k in range(n // width):
        slot = UPPER.index((k, k))
        diag = jnp.where(eye, packed[slot * width : (slot + 1) * width, :], 0.0)
        across.append(lax.rsqrt(jnp.sum(diag, axis=0, keepdims=True)))
        down.append(lax.rsqrt(jnp.sum(diag, axis=1, keepdims=True)))
        scale_ref[:, k * width : (k + 1) * width] = jnp.broadcast_to(across[k], (8, width))
    for slot, (p, q) in enumerate(UPPER):
        x_ref[p * width : (p + 1) * width, q * width : (q + 1) * width] = (
            packed[slot * width : (slot + 1) * width, :] * down[p] * across[q]
        )
    factor_steps(x_ref, 0, last)


def factor_open(place, half, other, n, last):
    return pl.pallas_call(
        functools.partial(factor_open_kernel, last),
        in_specs=[SMEM, VMEM, VMEM],
        out_specs=[VMEM] * 2,
        out_shape=[jax.ShapeDtypeStruct((n, n), F32), jax.ShapeDtypeStruct((8, n), F32)],
        scratch_shapes=[pltpu.VMEM((2 * half.shape[0], 128), F32)],
        compiler_params=params(),
        cost_estimate=cost(10 * last * n * n * n, 8 * n * n),
    )(place, half, other)


def factor_more_kernel(first, last, in_ref, x_ref):
    x_ref[...] = in_ref[...]
    factor_steps(x_ref, first, last)


def factor_more(value, first, last):
    n = value.shape[0]
    return pl.pallas_call(
        functools.partial(factor_more_kernel, first, last),
        in_specs=[VMEM],
        out_specs=VMEM,
        out_shape=jax.ShapeDtypeStruct((n, n), F32),
        compiler_params=params(),
        cost_estimate=cost(10 * (last - first) * n * n * n, 8 * n * n),
    )(value)


def lines_kernel(count, group, block, where_ref, *refs):
    tables, refs = refs[:count], refs[count:]
    factors, outs, top, rest = refs[:NX], refs[NX : 2 * NX], refs[-2], refs[-1]
    at = 0
    for table in tables:
        value = table[...]
        first = value.astype(jnp.bfloat16)
        top[at : at + table.shape[0], :] = first
        rest[at : at + table.shape[0], :] = (value - first.astype(F32)).astype(jnp.bfloat16)
        at += table.shape[0]
    lines, span = factors[0].shape
    links = span // block
    groups = lines // group
    for d in range(NX):

        def one(g, carry, d=d):
            at = [
                pl.multiple_of(where_ref[(d * groups + g) * links + t] * block, block) for t in range(links)
            ]
            line = pl.ds(pl.multiple_of(g * group, group), group)
            f = factors[d][line, :].astype(jnp.bfloat16)
            first = jnp.concatenate([top[pl.ds(a, block), :] for a in at], axis=0)
            second = jnp.concatenate([rest[pl.ds(a, block), :] for a in at], axis=0)
            outs[d][line, :] = jnp.dot(f, first, preferred_element_type=F32) + jnp.dot(
                f, second, preferred_element_type=F32
            )
            return carry

        lax.fori_loop(0, groups, one, 0, unroll=True)


def lines_part(where, tables, factors, group, block):
    rows, width = sum(t.shape[0] for t in tables), tables[0].shape[1]
    lines = factors[0].shape[0]
    return pl.pallas_call(
        functools.partial(lines_kernel, len(tables), group, block),
        in_specs=[SMEM] + [VMEM] * (len(tables) + NX),
        out_specs=[VMEM] * NX,
        out_shape=[jax.ShapeDtypeStruct((lines, width), F32)] * NX,
        scratch_shapes=[pltpu.VMEM((rows, width), jnp.bfloat16)] * 2,
        compiler_params=params(),
        cost_estimate=cost(64 * lines * width * NX * 256, 4 * rows * width),
    )(where, *tables, *factors)


def finish_kernel(scale, place_ref, *refs):
    ins, (x_ref, unit_ref, out_ref, wide) = refs[:NX], refs[NX:]
    width = ins[0].shape[1]
    me = place_ref[3]
    for d, r in enumerate(ins):
        wide[:, pl.ds(pl.multiple_of(lax.rem(me + d, NX) * width, width), width)] = r[...]
    pairs = []
    for value in (wide[...] * (scale * unit_ref[0:1, :]), x_ref[...]):
        top = value.astype(jnp.bfloat16)
        pairs.append((top, (value - top.astype(F32)).astype(jnp.bfloat16)))
    (a, a_rest), (b, b_rest) = pairs

    def product(p, q):
        return lax.dot_general(p, q, (((1,), (1,)), ((), ())), preferred_element_type=F32)

    out_ref[...] = product(a, b) + (product(a, b_rest) + product(a_rest, b))


def finish(place, parts, inverse, unit, scale):
    lines = parts[0].shape[0]
    n = inverse.shape[0]
    return pl.pallas_call(
        functools.partial(finish_kernel, scale),
        in_specs=[SMEM] + [VMEM] * (NX + 2),
        out_specs=VMEM,
        out_shape=jax.ShapeDtypeStruct((lines, n), F32),
        scratch_shapes=[pltpu.VMEM((lines, n), F32)],
        compiler_params=params(),
        cost_estimate=cost(12 * lines * n * n, 8 * n * n),
    )(place, *parts, inverse, unit)


def per_device(ensemble, probes, site_bus, incidence, shift_factors):
    sites = lax.axis_size("site")
    samps = lax.axis_size("samp")
    site = lax.axis_index("site")
    samp = lax.axis_index("samp")
    site_rows = ensemble.shape[0]
    n = probes.shape[1]
    block = site_rows // sites
    per = sites // samps
    half, x = samp // NX, samp % NX
    place = jnp.stack([site % NC, site // NC % NY, site // (NC * NY), x, half]).astype(jnp.int32)

    lines, span = shift_factors.shape
    groups, links = incidence.shape
    lists = jnp.pad(incidence.astype(F32), ((0, 0), (0, span - links)))
    carried = jnp.concatenate([shift_factors.astype(F32), lists], axis=0)

    owners = lax.dynamic_slice_in_dim(site_bus, site * sites, sites) // sites
    slot = jnp.arange(sites, dtype=jnp.int32)
    block_for = jnp.sum(jnp.where(owners[None, :] == slot[:, None], slot[None, :], 0), axis=1)

    def order_for(h):
        devices = h * NX + (x + jnp.arange(NX, dtype=jnp.int32)) % NX
        want = (devices[:, None] * per + jnp.arange(per, dtype=jnp.int32)[None, :]).reshape(-1)
        return jnp.sum(jnp.where(want[:, None] == slot[None, :], block_for[None, :], 0), axis=1)

    away = sketch_half(order_for(1 - half), ensemble, probes, block, 48)
    home = sketch_half(order_for(half), ensemble, probes, block, 48)
    sent = total_of(exchange(shift_x, away))
    crossed = swap_half(sent)
    around = [shift_x(home[d], d) for d in range(1, NX)]
    carried = exchange(shift_x, [after(carried, around)] * NX)
    cuts, send, keep = gram_parts(place, home[0], *around, after(crossed, carried[1:]))

    got = swap_core(send)
    pieces = add_and_split(place, 1, NY, [keep, got])
    cuts = exchange(shift_x, [after(c, pieces[0]) for c in cuts])
    part = total_of(exchange(shift_y, pieces))

    rows = len(cuts) * cuts[0].shape[0]
    blocks = turn(turn_y_kernel, place, [after(c, part) for c in cuts], [rows // NY] * NY, rows)
    parts = [part] + [shift_z(part, d) for d in range(1, NZL)]
    part = total_of([after(p, b) for p, b in zip(parts, blocks)])
    blocks = exchange(shift_y, blocks)

    part = part + swap_half(part)
    wide = jnp.concatenate([after(b, part) for b in blocks], axis=0)
    crossing = swap_half(wide)
    parts = [part] + [shift_x(part, d) for d in range(1, NX)]
    part = total_of([after(p, wide) for p in parts])

    parts = [part] + [shift_y(part, d) for d in range(1, NY)]
    blocks = turn(turn_z_kernel, place, [wide, after(crossing, part)], [2 * rows // NZL] * NZL, 2 * rows)
    run = join(place, 1, [after(p, b) for p, b in zip(parts, blocks)])
    blocks = exchange(shift_z, blocks)

    factors = [c[:lines] for c in carried]
    wanted = jnp.stack([c[lines:, :links] for c in carried]).astype(jnp.int32).reshape(-1)
    came_from = jnp.arange(sites * sites, dtype=jnp.int32) // sites
    source = jnp.sum(jnp.where(site_bus[None, :] == wanted[:, None], came_from[None, :], 0), axis=1)
    owner = wanted // sites
    dz = (owner // (NC * NY) - source // (NC * NY)) % NZL
    dy = (owner // NC - source // NC) % NY
    core = site % NC
    beside = jnp.where(core == 0, 1, sites - 1)
    offset = jnp.remainder(owner - site, sites)
    table_of = jnp.where(offset == 0, 0, jnp.where(offset == beside, 1, 2))
    far_core = (source % NC != core).astype(jnp.int32)
    place_of = jnp.where(table_of == 2, 4 + far_core, far_core * 2 + table_of)
    where = (place_of * NZL + dz) * NY + dy

    other = swap_core(run)
    inverse, unit = factor_open(place, run, other, n, 1)
    keep, pair, both = turn(
        functools.partial(turn_core_kernel, block), place, [after(b, inverse) for b in blocks], [rows, rows, 2 * rows]
    )
    tables = [keep, pair, swap_core(both), cross_chip(pair, True), cross_chip(keep, False)]
    inverse = factor_more(after(inverse, keep), 1, 3)
    parts = lines_part(where, [after(t, inverse) for t in tables], factors, lines // groups, block)
    parts = [parts[0]] + [shift_x(parts[d], -d) for d in range(1, NX)]
    inverse = factor_more(inverse, 3, 4)
    return finish(place, parts, inverse, unit, math.sqrt(site_rows * sites))


def solution(mesh):
    in_specs = (
        P("site", "samp"),
        P("samp", None),
        P(),
        P(("samp", "site"), None),
        P(("samp", "site"), None),
    )
    return jax.shard_map(
        per_device, mesh=mesh, in_specs=in_specs, out_specs=P(("samp", "site"), None), check_vma=False
    )
```
